32 devices in a mesh: rep: 4 (over x, core), fsdp: 8 (over z, y).
Axes of the slice: x: 2, y: 2, z: 4, core: 2. Of those that a mesh axis runs over, the one named last changes fastest.
Arguments:
- acts: bfloat16 [4, 2048, 8192], P('rep', 'fsdp'), may hold values from -6 to 6
- out_grad: bfloat16 [4, 2048, 512], P('rep', 'fsdp'), may hold values from -6 to 6
- weights: bfloat16 [4, 8192, 512], P('rep', 'fsdp'), may hold values from -0.0625 to 0.0625
- anchor: float32 [8192, 512], P('fsdp', 'rep'), may hold values from -0.0625 to 0.0625
- momentum: float32 [8192, 512], P('fsdp', 'rep'), may hold values from -0.078125 to 0.078125
- plan: int32 [4], replicated, may hold values 0 or 1
Outputs:
- values: bfloat16 [4, 2048, 512], P('rep', 'fsdp')
- act_grad: bfloat16 [4, 2048, 8192], P('rep', 'fsdp')
- new_weights: bfloat16 [4, 8192, 512], P('rep', 'fsdp')
- new_momentum: float32 [8192, 512], P('fsdp', 'rep')
The draws below stay inside these ranges and needn't reach their ends.
All inputs are finite; a program needn't handle non-finite values.
Results may differ from the reference program's by a relative error of at most 0.001.
Values may be sent and summed in bfloat16 or wider, within the bound.
A program may use at most 128 MiB of HBM per device.

```python
import math
import jax
import jax.numpy as jnp

D = 8192
HEADS_W = 4
HEAD_DIM = 128
KVW = 512
TOKENS = 2048
N_REP = 4


def plant(array, rng, smallest, top_value):
    spot = [jax.random.randint(jax.random.fold_in(rng, axis), (), 0, length) for axis, length in enumerate(array.shape)]
    main_axis = array.shape.index(max(array.shape))
    neighbour = spot[:main_axis] + [(spot[main_axis] + 1) % array.shape[main_axis]] + spot[main_axis + 1:]
    return array.at[tuple(spot)].set(smallest).at[tuple(neighbour)].set(top_value)


def with_spikes(values, rng, source, target, shards_of, factor):
    owner, partner = [(jnp.arange(values.shape[dim]) // (values.shape[dim] // shards_of)).reshape([-1 if axis == dim else 1 for axis in range(values.ndim)]) for dim in (source, target)]
    chosen = jax.random.permutation(rng, shards_of)[partner]
    strong = (owner == chosen) | (owner == (partner + shards_of // 2) % shards_of)
    return jnp.where(strong, factor * values, values)


def level_of(rng, extent, cuts, low, high):
    level, own = 1.0, jax.random.fold_in(rng, 6)
    for axis_at, shards_of in cuts:
        draws = jnp.exp(jax.random.uniform(jax.random.fold_in(own, axis_at), (shards_of,), jnp.float32, low / len(cuts), high / len(cuts)))
        level = level * jnp.repeat(draws, extent[axis_at] // shards_of).reshape([-1 if axis == axis_at else 1 for axis in range(len(extent))])
    return level


def bell_draw(rng, dims, width, reach, split=(), dtype=jnp.bfloat16):
    loudness = level_of(rng, dims, split, -0.22, 0.18) if split else 1.0
    drawn = jax.random.normal(rng, dims, jnp.float32) * width * loudness
    return jnp.minimum(jnp.maximum(drawn, -reach), reach).astype(dtype)


def heavy_noise(stream_key, shape, deviation, most, pieces, heavy, dtype=jnp.bfloat16):
    drawn = deviation * jax.random.normal(stream_key, shape, jnp.float32)
    if pieces:
        drawn = drawn * level_of(stream_key, shape, pieces, -0.22, 0.18)
    return jnp.clip(with_spikes(drawn, jax.random.fold_in(stream_key, 3), *heavy), -most, most).astype(dtype)


def setup_inputs(seed: int = 0) -> dict:
    key_list = jax.random.split(jax.random.key(seed), 7)
    return {
        "acts": heavy_noise(key_list[0], (N_REP, TOKENS, D), 1.0, 6.0, ((0, 4), (1, 8)), (1, 2, 8, 2.0)),
        "out_grad": bell_draw(key_list[1], (N_REP, TOKENS, KVW), 1.0, 6.0, ((0, 4), (1, 8))),
        "weights": bell_draw(key_list[2], (N_REP, D, KVW), D ** -0.5, 0.0625, ((0, 4), (1, 8))),
        "anchor": bell_draw(key_list[3], (D, KVW), D ** -0.5, 0.0625, ((0, 8), (1, 4)), jnp.float32),
        "momentum": bell_draw(key_list[4], (D, KVW), (0.5 * D ** -0.5), 0.078125, ((0, 8), (1, 4)), jnp.float32),
        "plan": plant((jax.random.randint(key_list[5], (HEADS_W,), 0, 2) < 1).astype(jnp.int32), jax.random.fold_in(key_list[5], 1), 0, 1),
    }


outer_rate = 0.7
momentum_coef = 0.9

def reference(acts, out_grad, weights, anchor, momentum, plan):
    inner_rate = 1.0 / math.sqrt(TOKENS * D)
    value_list = []
    grad_list = []
    inner_list = []
    for group in range(N_REP):
        value_list.append(jnp.dot(acts[group], weights[group], preferred_element_type=jnp.float32).astype(jnp.bfloat16))
        grad_list.append(jnp.dot(out_grad[group], weights[group].T, preferred_element_type=jnp.float32).astype(jnp.bfloat16))
        weight_grad = jnp.dot(acts[group].T, out_grad[group], preferred_element_type=jnp.float32)
        inner_list.append(weights[group].astype(jnp.float32) - inner_rate * weight_grad)
    group_total = inner_list[0]
    for group in range(1, N_REP):
        group_total = group_total + inner_list[group]
    group_mean = group_total / N_REP
    pseudo_grad = anchor - group_mean
    mom_next = momentum_coef * momentum + pseudo_grad
    outer_weight = anchor - outer_rate * (pseudo_grad + momentum_coef * mom_next)
    col_mask = jnp.repeat(plan, HEAD_DIM) > 0
    outer_bf = outer_weight.astype(jnp.bfloat16)
    new_list = [jnp.where(col_mask[None, :], outer_bf, inner_weight.astype(jnp.bfloat16)) for inner_weight in inner_list]
    new_momentum = jnp.where(col_mask[None, :], mom_next, momentum)
    return (jnp.stack(value_list), jnp.stack(grad_list), jnp.stack(new_list), new_momentum)
```

```python
import functools
import math

import jax
import jax.numpy as jnp
from jax import lax
from jax.experimental import pallas as pl
from jax.experimental.pallas import tpu as pltpu
from jax.sharding import PartitionSpec as P

outer_rate = 0.7
momentum_coef = 0.9
MESH = pl.DeviceIdType.MESH
F32 = jnp.float32
BF16 = jnp.bfloat16
LEFT, RIGHT, PARTNER = 0, 1, 2


def kernel(
    n, groups, chunks, rate,
    plan, acts_hbm, og_hbm, w_hbm, anchor_hbm, mom_hbm,
    values_out, ag_hbm, new_w_out, new_mom_out,
    acts, acts_t, og_all, w_all, ag, vals, wgrad, inner, rep_in, outer_in, anchor, mom,
    acts_sem, og_sem, w_sem, state_sem, ag_sem,
    og_send, og_recv, w_send, w_recv, a_send, a_recv,
    r_send, r_recv, o_send, o_recv,
):
    me = lax.axis_index("fsdp")
    rep = lax.axis_index("rep")
    line = n // 2
    z = me // 2
    y = lax.rem(me, 2)
    width = acts.shape[2]
    rows = w_all.shape[2]
    block = anchor.shape[1]

    def cols(s):
        return pl.ds(pl.multiple_of(s * width, width), width)

    def load_acts(s):
        return pltpu.make_async_copy(acts_hbm.at[:, cols(s)], acts.at[s], acts_sem.at[s])

    def load_w(c):
        return pltpu.make_async_copy(
            w_hbm.at[pl.ds(c * rows, rows)], w_all.at[me, c], w_sem.at[c]
        )

    load_og = pltpu.make_async_copy(og_hbm, og_all.at[me], og_sem.at[0])
    load_anchor = pltpu.make_async_copy(anchor_hbm, anchor, state_sem.at[0])
    load_mom = pltpu.make_async_copy(mom_hbm, mom, state_sem.at[1])
    load_og.start()
    for c in range(chunks):
        load_w(c).start()

    @pl.loop(0, n)
    def _(s):
        load_acts(s).start()

    load_anchor.start()
    load_mom.start()

    barrier = pltpu.get_barrier_semaphore()

    @pl.loop(1, n)
    def _(k):
        pl.semaphore_signal(
            barrier, inc=1, device_id={"fsdp": lax.rem(me + k, n)}, device_id_type=MESH
        )

    @pl.loop(1, groups)
    def _(k):
        pl.semaphore_signal(
            barrier, inc=1, device_id={"rep": lax.rem(rep + k, groups)}, device_id_type=MESH
        )

    pl.semaphore_wait(barrier, n - 1 + groups - 1)

    def target(way):
        return (jnp.maximum(me - 2, 0), jnp.minimum(me + 2, n - 1), me + 1 - 2 * y)[way]

    def og_copy(s, way):
        return pltpu.make_async_remote_copy(
            src_ref=og_all.at[s], dst_ref=og_all.at[s],
            send_sem=og_send.at[s, way], recv_sem=og_recv.at[s],
            device_id={"fsdp": target(way)}, device_id_type=MESH,
        )

    def w_copy(c):
        def make(s, way):
            return pltpu.make_async_remote_copy(
                src_ref=w_all.at[s, c], dst_ref=w_all.at[s, c],
                send_sem=w_send.at[s, c, way], recv_sem=w_recv.at[s, c],
                device_id={"fsdp": target(way)}, device_id_type=MESH,
            )
        return make

    def own(make, act):
        s = me
        pl.when(z > 0)(lambda: act(make(s, LEFT)))
        pl.when(z < line - 1)(lambda: act(make(s, RIGHT)))
        act(make(s, PARTNER))

    def forward(make, k, act, wait):
        @pl.when(z >= k)
        def _():
            s = me - 2 * k
            if wait:
                make(s, PARTNER).wait_recv()
            pl.when(z < line - 1)(lambda: act(make(s, RIGHT)))
            act(make(s, PARTNER))

        @pl.when(z + k < line)
        def _():
            s = me + 2 * k
            if wait:
                make(s, PARTNER).wait_recv()
            pl.when(z > 0)(lambda: act(make(s, LEFT)))
            act(make(s, PARTNER))

    def start(copy):
        copy.start()

    def wait_send(copy):
        copy.wait_send()

    def a_copy(k):
        d = lax.rem(me + k, n)
        return pltpu.make_async_remote_copy(
            src_ref=acts_hbm.at[:, cols(d)], dst_ref=acts_t.at[me],
            send_sem=a_send.at[k], recv_sem=a_recv.at[me],
            device_id={"fsdp": d}, device_id_type=MESH,
        )

    def a_arrived(s):
        return pltpu.make_async_remote_copy(
            src_ref=acts_hbm.at[:, cols(s)], dst_ref=acts_t.at[s],
            send_sem=a_send.at[0], recv_sem=a_recv.at[s],
            device_id={"fsdp": lax.rem(me + 1, n)}, device_id_type=MESH,
        )

    load_og.wait()
    own(og_copy, start)

    @pl.loop(1, n)
    def _(k):
        a_copy(k).start()

    for c in range(chunks):
        load_w(c).wait()
        own(w_copy(c), start)

    def ag_store(s):
        return pltpu.make_async_copy(ag.at[s], ag_hbm.at[:, cols(s)], ag_sem.at[s])

    def use_weight(s):
        for c in range(chunks):
            part = slice(c * rows, (c + 1) * rows)
            vals[...] += jnp.dot(acts[s, :, part], w_all[s, c], preferred_element_type=F32)
            ag[s, :, part] = lax.dot_general(
                og_all[me], w_all[s, c], (((1,), (1,)), ((), ())), preferred_element_type=F32
            ).astype(BF16)
        ag_store(s).start()

    def use_acts(a, s):
        wgrad[...] += lax.dot_general(
            a, og_all[s], (((0,), (0,)), ((), ())), preferred_element_type=F32
        )

    vals[...] = jnp.zeros_like(vals)
    wgrad[...] = jnp.zeros_like(wgrad)

    @pl.loop(0, n)
    def _(s):
        load_acts(s).wait()

    @pl.loop(1, line)
    def _(k):
        forward(og_copy, k, start, True)

    use_weight(me)
    use_acts(acts[me], me)

    def gather(k):
        for c in range(chunks):
            forward(w_copy(c), k, start, True)

    def use_line(k):
        @pl.loop(0, 2)
        def _(j):
            zz = z + (1 - 2 * j) * k

            @pl.when((zz >= 0) & (zz < line))
            def _():
                use_weight(zz * 2 + y)

    def use_partner(k):
        @pl.loop(0, 2)
        def _(j):
            zz = z + (1 - 2 * j) * k

            @pl.when((zz >= 0) & (zz < line) & ((k > 0) | (j == 0)))
            def _():
                s = zz * 2 + 1 - y
                for c in range(chunks):
                    w_copy(c)(s, PARTNER).wait_recv()
                use_weight(s)

    gather(1)

    @pl.loop(0, line)
    def _(zz):
        og_copy(zz * 2 + 1 - y, PARTNER).wait_recv()

    @pl.loop(1, n)
    def _(k):
        s = lax.rem(me + n - k, n)
        a_arrived(s).wait_recv()
        use_acts(acts_t[s], s)

    for j in range(groups):
        part = slice(j * block, (j + 1) * block)
        for c in range(chunks):
            across = slice(c * rows, (c + 1) * rows)
            inner[j, across] = (
                w_all[me, c, :, part].astype(F32) - rate * wgrad[across, part]
            )

    def r_copy(k):
        d = lax.rem(rep + k, groups)
        return pltpu.make_async_remote_copy(
            src_ref=inner.at[d], dst_ref=rep_in.at[rep],
            send_sem=r_send.at[k], recv_sem=r_recv.at[rep],
            device_id={"rep": d}, device_id_type=MESH,
        )

    def r_arrived(k):
        d = lax.rem(rep + k, groups)
        return pltpu.make_async_remote_copy(
            src_ref=inner.at[d], dst_ref=rep_in.at[d],
            send_sem=r_send.at[k], recv_sem=r_recv.at[d],
            device_id={"rep": d}, device_id_type=MESH,
        )

    def o_copy(k):
        d = lax.rem(rep + k, groups)
        return pltpu.make_async_remote_copy(
            src_ref=outer_in.at[rep], dst_ref=outer_in.at[rep],
            send_sem=o_send.at[k], recv_sem=o_recv.at[rep],
            device_id={"rep": d}, device_id_type=MESH,
        )

    def o_arrived(k):
        d = lax.rem(rep + k, groups)
        return pltpu.make_async_remote_copy(
            src_ref=outer_in.at[d], dst_ref=outer_in.at[d],
            send_sem=o_send.at[k], recv_sem=o_recv.at[d],
            device_id={"rep": d}, device_id_type=MESH,
        )

    for k in range(1, groups):
        r_copy(k).start()
    rep_in[rep] = inner[rep]

    use_line(1)
    use_partner(0)

    @pl.loop(2, line)
    def _(k):
        gather(k)
        use_line(k)
        use_partner(k - 1)

    for k in range(1, groups):
        r_arrived(k).wait_recv()
    load_anchor.wait()
    load_mom.wait()
    total = rep_in[0]
    for j in range(1, groups):
        total = total + rep_in[j]
    pseudo_grad = anchor[...] - total / groups
    mom_next = momentum_coef * mom[...] + pseudo_grad
    outer_in[rep] = (
        anchor[...] - outer_rate * (pseudo_grad + momentum_coef * mom_next)
    ).astype(BF16)
    for k in range(1, groups):
        o_copy(k).start()
    synced = jnp.full(mom_next.shape, plan[rep], jnp.int32) > 0
    new_mom_out[...] = jnp.where(synced, mom_next, mom[...])

    use_partner(line - 1)
    values_out[...] = vals[...].astype(BF16)

    for k in range(1, groups):
        o_arrived(k).wait_recv()
    for j in range(groups):
        synced = jnp.full(inner.shape[1:], plan[j], jnp.int32) > 0
        new_w_out[:, j * block:(j + 1) * block] = jnp.where(
            synced, outer_in[j].astype(F32), inner[j]
        ).astype(BF16)

    own(og_copy, wait_send)
    for c in range(chunks):
        own(w_copy(c), wait_send)

    @pl.loop(1, line)
    def _(k):
        forward(og_copy, k, wait_send, False)
        for c in range(chunks):
            forward(w_copy(c), k, wait_send, False)

    @pl.loop(1, n)
    def _(k):
        a_copy(k).wait_send()

    for k in range(1, groups):
        r_copy(k).wait_send()
        o_copy(k).wait_send()

    @pl.loop(0, n)
    def _(s):
        ag_store(s).wait()


def local(n, groups, acts, out_grad, weights, anchor, momentum, plan):
    tokens, depth = acts.shape[1:]
    rows, kvw = weights.shape[1:]
    block = anchor.shape[1]
    rate = 1.0 / math.sqrt(tokens * n * depth)
    chunks = 2
    any_spec = pl.BlockSpec(memory_space=pl.ANY)
    vmem = pl.BlockSpec(memory_space=pltpu.VMEM)
    dma = pltpu.SemaphoreType.DMA
    values, act_grad, new_w, new_mom = pl.pallas_call(
        functools.partial(kernel, n, groups, chunks, rate),
        out_shape=(
            jax.ShapeDtypeStruct((tokens, kvw), BF16),
            jax.ShapeDtypeStruct((tokens, depth), BF16),
            jax.ShapeDtypeStruct((rows, kvw), BF16),
            jax.ShapeDtypeStruct((rows, block), F32),
        ),
        in_specs=[pl.BlockSpec(memory_space=pltpu.SMEM)] + [any_spec] * 5,
        out_specs=(vmem, any_spec, vmem, vmem),
        scratch_shapes=[
            pltpu.VMEM((n, tokens, rows), BF16),
            pltpu.VMEM((n, tokens, rows), BF16),
            pltpu.VMEM((n, tokens, kvw), BF16),
            pltpu.VMEM((n, chunks, rows // chunks, kvw), BF16),
            pltpu.VMEM((n, tokens, rows), BF16),
            pltpu.VMEM((tokens, kvw), F32),
            pltpu.VMEM((rows, kvw), F32),
            pltpu.VMEM((groups, rows, block), F32),
            pltpu.VMEM((groups, rows, block), F32),
            pltpu.VMEM((groups, rows, block), BF16),
            pltpu.VMEM((rows, block), F32),
            pltpu.VMEM((rows, block), F32),
            dma((n,)), dma((1,)), dma((chunks,)), dma((2,)), dma((n,)),
            dma((n, 3)), dma((n,)), dma((n, chunks, 3)), dma((n, chunks)), dma((n,)), dma((n,)),
            dma((groups,)), dma((groups,)), dma((groups,)), dma((groups,)),
        ],
        compiler_params=pltpu.CompilerParams(
            collective_id=0, has_side_effects=True, vmem_limit_bytes=56 * 2**20
        ),
        cost_estimate=pl.CostEstimate(
            flops=6 * tokens * depth * kvw, bytes_accessed=24 * 2**20, transcendentals=0
        ),
    )(plan, acts[0], out_grad[0], weights[0], anchor, momentum)
    return values[None], act_grad[None], new_w[None], new_mom


def solution(mesh):
    placed = (
        P("rep", "fsdp", None),
        P("rep", "fsdp", None),
        P("rep", "fsdp", None),
        P("fsdp", "rep"),
        P("fsdp", "rep"),
        P(),
    )
    return jax.shard_map(
        functools.partial(local, mesh.shape["fsdp"], mesh.shape["rep"]),
        mesh=mesh,
        in_specs=placed,
        out_specs=(
            P("rep", "fsdp", None),
            P("rep", "fsdp", None),
            P("rep", "fsdp", None),
            P("fsdp", "rep"),
        ),
        check_vma=False,
    )
```

```python
import functools
import math

import jax
import jax.numpy as jnp
from jax import lax
from jax.experimental import pallas as pl
from jax.experimental.pallas import tpu as pltpu
from jax.sharding import PartitionSpec as P

outer_rate = 0.7
momentum_coef = 0.9
MESH = pl.DeviceIdType.MESH
F32 = jnp.float32
BF16 = jnp.bfloat16
LEFT, RIGHT, PARTNER = 0, 1, 2


def kernel(
    n, groups, chunks, rate,
    plan, acts_hbm, og_hbm, w_hbm, anchor_hbm, mom_hbm,
    values_out, ag_hbm, new_w_out, new_mom_out,
    acts, acts_t, og_all, w_all, ag, vals, wgrad, inner, rep_in, outer_in, anchor, mom,
    acts_sem, og_sem, w_sem, state_sem, ag_sem,
    og_send, og_recv, w_send, w_recv, a_send, a_recv,
    r_send, r_recv, o_send, o_recv,
):
    me = lax.axis_index("fsdp")
    rep = lax.axis_index("rep")
    line = n // 2
    z = me // 2
    y = lax.rem(me, 2)
    width = acts.shape[2]
    rows = w_all.shape[2]
    block = anchor.shape[1]

    def cols(s):
        return pl.ds(pl.multiple_of(s * width, width), width)

    def load_acts(s):
        return pltpu.make_async_copy(acts_hbm.at[:, cols(s)], acts.at[s], acts_sem.at[s])

    def load_w(c):
        return pltpu.make_async_copy(
            w_hbm.at[pl.ds(c * rows, rows)], w_all.at[me, c], w_sem.at[c]
        )

    load_og = pltpu.make_async_copy(og_hbm, og_all.at[me], og_sem.at[0])
    load_anchor = pltpu.make_async_copy(anchor_hbm, anchor, state_sem.at[0])
    load_mom = pltpu.make_async_copy(mom_hbm, mom, state_sem.at[1])
    load_og.start()
    for c in range(chunks):
        load_w(c).start()

    @pl.loop(0, n)
    def _(s):
        load_acts(s).start()

    load_anchor.start()
    load_mom.start()

    barrier = pltpu.get_barrier_semaphore()

    @pl.loop(1, n)
    def _(k):
        pl.semaphore_signal(
            barrier, inc=1, device_id={"fsdp": lax.rem(me + k, n)}, device_id_type=MESH
        )

    @pl.loop(1, groups)
    def _(k):
        pl.semaphore_signal(
            barrier, inc=1, device_id={"rep": lax.rem(rep + k, groups)}, device_id_type=MESH
        )

    pl.semaphore_wait(barrier, n - 1 + groups - 1)

    def target(way):
        return (jnp.maximum(me - 2, 0), jnp.minimum(me + 2, n - 1), me + 1 - 2 * y)[way]

    def og_copy(s, way):
        return pltpu.make_async_remote_copy(
            src_ref=og_all.at[s], dst_ref=og_all.at[s],
            send_sem=og_send.at[s, way], recv_sem=og_recv.at[s],
            device_id={"fsdp": target(way)}, device_id_type=MESH,
        )

    def w_copy(c):
        def make(s, way):
            return pltpu.make_async_remote_copy(
                src_ref=w_all.at[s, c], dst_ref=w_all.at[s, c],
                send_sem=w_send.at[s, c, way], recv_sem=w_recv.at[s, c],
                device_id={"fsdp": target(way)}, device_id_type=MESH,
            )
        return make

    def own(make, act):
        s = me
        pl.when(z > 0)(lambda: act(make(s, LEFT)))
        pl.when(z < line - 1)(lambda: act(make(s, RIGHT)))
        act(make(s, PARTNER))

    def forward(make, k, act, wait):
        @pl.when(z >= k)
        def _():
            s = me - 2 * k
            if wait:
                make(s, PARTNER).wait_recv()
            pl.when(z < line - 1)(lambda: act(make(s, RIGHT)))
            act(make(s, PARTNER))

        @pl.when(z + k < line)
        def _():
            s = me + 2 * k
            if wait:
                make(s, PARTNER).wait_recv()
            pl.when(z > 0)(lambda: act(make(s, LEFT)))
            act(make(s, PARTNER))

    def start(copy):
        copy.start()

    def wait_send(copy):
        copy.wait_send()

    def a_copy(k):
        d = lax.rem(me + k, n)
        return pltpu.make_async_remote_copy(
            src_ref=acts_hbm.at[:, cols(d)], dst_ref=acts_t.at[me],
            send_sem=a_send.at[k], recv_sem=a_recv.at[me],
            device_id={"fsdp": d}, device_id_type=MESH,
        )

    def a_arrived(s):
        return pltpu.make_async_remote_copy(
            src_ref=acts_hbm.at[:, cols(s)], dst_ref=acts_t.at[s],
            send_sem=a_send.at[0], recv_sem=a_recv.at[s],
            device_id={"fsdp": lax.rem(me + 1, n)}, device_id_type=MESH,
        )

    load_og.wait()
    own(og_copy, start)

    for c in range(chunks):
        load_w(c).wait()
        own(w_copy(c), start)

    @pl.loop(1, n)
    def _(k):
        a_copy(k).start()

    def ag_store(s):
        return pltpu.make_async_copy(ag.at[s], ag_hbm.at[:, cols(s)], ag_sem.at[s])

    def use_weight(s):
        for c in range(chunks):
            part = slice(c * rows, (c + 1) * rows)
            vals[...] += jnp.dot(acts[s, :, part], w_all[s, c], preferred_element_type=F32)
            ag[s, :, part] = lax.dot_general(
                og_all[me], w_all[s, c], (((1,), (1,)), ((), ())), preferred_element_type=F32
            ).astype(BF16)
        ag_store(s).start()

    def use_acts(a, s):
        wgrad[...] += lax.dot_general(
            a, og_all[s], (((0,), (0,)), ((), ())), preferred_element_type=F32
        )

    vals[...] = jnp.zeros_like(vals)
    wgrad[...] = jnp.zeros_like(wgrad)

    @pl.loop(0, n)
    def _(s):
        load_acts(s).wait()

    @pl.loop(1, line)
    def _(k):
        forward(og_copy, k, start, True)

    use_weight(me)
    use_acts(acts[me], me)

    def gather(k):
        for c in range(chunks):
            forward(w_copy(c), k, start, True)

    def use_line(k):
        @pl.loop(0, 2)
        def _(j):
            zz = z + (1 - 2 * j) * k

            @pl.when((zz >= 0) & (zz < line))
            def _():
                use_weight(zz * 2 + y)

    def use_partner(k):
        @pl.loop(0, 2)
        def _(j):
            zz = z + (1 - 2 * j) * k

            @pl.when((zz >= 0) & (zz < line) & ((k > 0) | (j == 0)))
            def _():
                s = zz * 2 + 1 - y
                for c in range(chunks):
                    w_copy(c)(s, PARTNER).wait_recv()
                use_weight(s)

    ahead = max(line - 2, 1)

    @pl.loop(1, ahead + 1)
    def _(k):
        gather(k)

    @pl.loop(0, line)
    def _(zz):
        og_copy(zz * 2 + 1 - y, PARTNER).wait_recv()

    @pl.loop(1, n)
    def _(k):
        s = lax.rem(me + n - k, n)
        a_arrived(s).wait_recv()
        use_acts(acts_t[s], s)

    for j in range(groups):
        part = slice(j * block, (j + 1) * block)
        for c in range(chunks):
            across = slice(c * rows, (c + 1) * rows)
            inner[j, across] = (
                w_all[me, c, :, part].astype(F32) - rate * wgrad[across, part]
            )

    def r_copy(k):
        d = lax.rem(rep + k, groups)
        return pltpu.make_async_remote_copy(
            src_ref=inner.at[d], dst_ref=rep_in.at[rep],
            send_sem=r_send.at[k], recv_sem=r_recv.at[rep],
            device_id={"rep": d}, device_id_type=MESH,
        )

    def r_arrived(k):
        d = lax.rem(rep + k, groups)
        return pltpu.make_async_remote_copy(
            src_ref=inner.at[d], dst_ref=rep_in.at[d],
            send_sem=r_send.at[k], recv_sem=r_recv.at[d],
            device_id={"rep": d}, device_id_type=MESH,
        )

    def o_copy(k):
        d = lax.rem(rep + k, groups)
        return pltpu.make_async_remote_copy(
            src_ref=outer_in.at[rep], dst_ref=outer_in.at[rep],
            send_sem=o_send.at[k], recv_sem=o_recv.at[rep],
            device_id={"rep": d}, device_id_type=MESH,
        )

    def o_arrived(k):
        d = lax.rem(rep + k, groups)
        return pltpu.make_async_remote_copy(
            src_ref=outer_in.at[d], dst_ref=outer_in.at[d],
            send_sem=o_send.at[k], recv_sem=o_recv.at[d],
            device_id={"rep": d}, device_id_type=MESH,
        )

    for k in range(1, groups):
        r_copy(k).start()
    rep_in[rep] = inner[rep]

    @pl.loop(ahead + 1, line)
    def _(k):
        gather(k)

    use_partner(0)

    @pl.loop(1, line - 1)
    def _(k):
        use_line(k)
        use_partner(k)

    for k in range(1, groups):
        r_arrived(k).wait_recv()
    load_anchor.wait()
    load_mom.wait()
    total = rep_in[0]
    for j in range(1, groups):
        total = total + rep_in[j]
    pseudo_grad = anchor[...] - total / groups
    mom_next = momentum_coef * mom[...] + pseudo_grad
    outer_in[rep] = (
        anchor[...] - outer_rate * (pseudo_grad + momentum_coef * mom_next)
    ).astype(BF16)
    for k in range(1, groups):
        o_copy(k).start()
    synced = jnp.full(mom_next.shape, plan[rep], jnp.int32) > 0
    new_mom_out[...] = jnp.where(synced, mom_next, mom[...])

    use_line(line - 1)
    use_partner(line - 1)
    values_out[...] = vals[...].astype(BF16)

    for k in range(1, groups):
        o_arrived(k).wait_recv()
    for j in range(groups):
        synced = jnp.full(inner.shape[1:], plan[j], jnp.int32) > 0
        new_w_out[:, j * block:(j + 1) * block] = jnp.where(
            synced, outer_in[j].astype(F32), inner[j]
        ).astype(BF16)

    own(og_copy, wait_send)
    for c in range(chunks):
        own(w_copy(c), wait_send)

    @pl.loop(1, line)
    def _(k):
        forward(og_copy, k, wait_send, False)
        for c in range(chunks):
            forward(w_copy(c), k, wait_send, False)

    @pl.loop(1, n)
    def _(k):
        a_copy(k).wait_send()

    for k in range(1, groups):
        r_copy(k).wait_send()
        o_copy(k).wait_send()

    @pl.loop(0, n)
    def _(s):
        ag_store(s).wait()


def local(n, groups, acts, out_grad, weights, anchor, momentum, plan):
    tokens, depth = acts.shape[1:]
    rows, kvw = weights.shape[1:]
    block = anchor.shape[1]
    rate = 1.0 / math.sqrt(tokens * n * depth)
    chunks = 2
    any_spec = pl.BlockSpec(memory_space=pl.ANY)
    vmem = pl.BlockSpec(memory_space=pltpu.VMEM)
    dma = pltpu.SemaphoreType.DMA
    values, act_grad, new_w, new_mom = pl.pallas_call(
        functools.partial(kernel, n, groups, chunks, rate),
        out_shape=(
            jax.ShapeDtypeStruct((tokens, kvw), BF16),
            jax.ShapeDtypeStruct((tokens, depth), BF16),
            jax.ShapeDtypeStruct((rows, kvw), BF16),
            jax.ShapeDtypeStruct((rows, block), F32),
        ),
        in_specs=[pl.BlockSpec(memory_space=pltpu.SMEM)] + [any_spec] * 5,
        out_specs=(vmem, any_spec, vmem, vmem),
        scratch_shapes=[
            pltpu.VMEM((n, tokens, rows), BF16),
            pltpu.VMEM((n, tokens, rows), BF16),
            pltpu.VMEM((n, tokens, kvw), BF16),
            pltpu.VMEM((n, chunks, rows // chunks, kvw), BF16),
            pltpu.VMEM((n, tokens, rows), BF16),
            pltpu.VMEM((tokens, kvw), F32),
            pltpu.VMEM((rows, kvw), F32),
            pltpu.VMEM((groups, rows, block), F32),
            pltpu.VMEM((groups, rows, block), F32),
            pltpu.VMEM((groups, rows, block), BF16),
            pltpu.VMEM((rows, block), F32),
            pltpu.VMEM((rows, block), F32),
            dma((n,)), dma((1,)), dma((chunks,)), dma((2,)), dma((n,)),
            dma((n, 3)), dma((n,)), dma((n, chunks, 3)), dma((n, chunks)), dma((n,)), dma((n,)),
            dma((groups,)), dma((groups,)), dma((groups,)), dma((groups,)),
        ],
        compiler_params=pltpu.CompilerParams(
            collective_id=0, has_side_effects=True, vmem_limit_bytes=56 * 2**20
        ),
        cost_estimate=pl.CostEstimate(
            flops=6 * tokens * depth * kvw, bytes_accessed=24 * 2**20, transcendentals=0
        ),
    )(plan, acts[0], out_grad[0], weights[0], anchor, momentum)
    return values[None], act_grad[None], new_w[None], new_mom


def solution(mesh):
    placed = (
        P("rep", "fsdp", None),
        P("rep", "fsdp", None),
        P("rep", "fsdp", None),
        P("fsdp", "rep"),
        P("fsdp", "rep"),
        P(),
    )
    return jax.shard_map(
        functools.partial(local, mesh.shape["fsdp"], mesh.shape["rep"]),
        mesh=mesh,
        in_specs=placed,
        out_specs=(
            P("rep", "fsdp", None),
            P("rep", "fsdp", None),
            P("rep", "fsdp", None),
            P("fsdp", "rep"),
        ),
        check_vma=False,
    )
```

```python
import functools
import math

import jax
import jax.numpy as jnp
from jax import lax
from jax.experimental import pallas as pl
from jax.experimental.pallas import tpu as pltpu
from jax.sharding import PartitionSpec as P

outer_rate = 0.7
momentum_coef = 0.9
MESH = pl.DeviceIdType.MESH
F32 = jnp.float32
BF16 = jnp.bfloat16
LEFT, RIGHT, PARTNER = 0, 1, 2


def kernel(
    n, groups, chunks, rate,
    plan, acts_hbm, og_hbm, w_hbm, anchor_hbm, mom_hbm,
    values_out, ag_hbm, new_w_out, new_mom_out,
    acts, acts_t, og_all, w_all, ag, vals, wgrad, inner, rep_in, outer_in, anchor, mom,
    acts_sem, og_sem, w_sem, state_sem, ag_sem,
    og_send, og_recv, w_send, w_recv, a_send, a_recv,
    r_send, r_recv, o_send, o_recv,
):
    me = lax.axis_index("fsdp")
    rep = lax.axis_index("rep")
    line = n // 2
    z = me // 2
    y = lax.rem(me, 2)
    width = acts.shape[2]
    rows = w_all.shape[2]
    block = anchor.shape[1]

    def cols(s):
        return pl.ds(pl.multiple_of(s * width, width), width)

    def load_acts(s):
        return pltpu.make_async_copy(acts_hbm.at[:, cols(s)], acts.at[s], acts_sem.at[s])

    def load_w(c):
        return pltpu.make_async_copy(
            w_hbm.at[pl.ds(c * rows, rows)], w_all.at[me, c], w_sem.at[c]
        )

    load_og = pltpu.make_async_copy(og_hbm, og_all.at[me], og_sem.at[0])
    load_anchor = pltpu.make_async_copy(anchor_hbm, anchor, state_sem.at[0])
    load_mom = pltpu.make_async_copy(mom_hbm, mom, state_sem.at[1])
    load_og.start()
    for c in range(chunks):
        load_w(c).start()

    @pl.loop(0, n)
    def _(s):
        load_acts(s).start()

    load_anchor.start()
    load_mom.start()

    barrier = pltpu.get_barrier_semaphore()

    @pl.loop(1, n)
    def _(k):
        pl.semaphore_signal(
            barrier, inc=1, device_id={"fsdp": lax.rem(me + k, n)}, device_id_type=MESH
        )

    @pl.loop(1, groups)
    def _(k):
        pl.semaphore_signal(
            barrier, inc=1, device_id={"rep": lax.rem(rep + k, groups)}, device_id_type=MESH
        )

    pl.semaphore_wait(barrier, n - 1 + groups - 1)

    def target(way):
        return (jnp.maximum(me - 2, 0), jnp.minimum(me + 2, n - 1), me + 1 - 2 * y)[way]

    def og_copy(s, way):
        return pltpu.make_async_remote_copy(
            src_ref=og_all.at[s], dst_ref=og_all.at[s],
            send_sem=og_send.at[s, way], recv_sem=og_recv.at[s],
            device_id={"fsdp": target(way)}, device_id_type=MESH,
        )

    def w_copy(c):
        def make(s, way):
            return pltpu.make_async_remote_copy(
                src_ref=w_all.at[s, c], dst_ref=w_all.at[s, c],
                send_sem=w_send.at[s, c, way], recv_sem=w_recv.at[s, c],
                device_id={"fsdp": target(way)}, device_id_type=MESH,
            )
        return make

    def own(make, act):
        s = me
        pl.when(z > 0)(lambda: act(make(s, LEFT)))
        pl.when(z < line - 1)(lambda: act(make(s, RIGHT)))
        act(make(s, PARTNER))

    def forward(make, k, act, wait):
        @pl.when(z >= k)
        def _():
            s = me - 2 * k
            if wait:
                make(s, PARTNER).wait_recv()
            pl.when(z < line - 1)(lambda: act(make(s, RIGHT)))
            act(make(s, PARTNER))

        @pl.when(z + k < line)
        def _():
            s = me + 2 * k
            if wait:
                make(s, PARTNER).wait_recv()
            pl.when(z > 0)(lambda: act(make(s, LEFT)))
            act(make(s, PARTNER))

    def start(copy):
        copy.start()

    def wait_send(copy):
        copy.wait_send()

    def a_copy(k):
        d = lax.rem(me + k, n)
        return pltpu.make_async_remote_copy(
            src_ref=acts_hbm.at[:, cols(d)], dst_ref=acts_t.at[me],
            send_sem=a_send.at[k], recv_sem=a_recv.at[me],
            device_id={"fsdp": d}, device_id_type=MESH,
        )

    def a_arrived(s):
        return pltpu.make_async_remote_copy(
            src_ref=acts_hbm.at[:, cols(s)], dst_ref=acts_t.at[s],
            send_sem=a_send.at[0], recv_sem=a_recv.at[s],
            device_id={"fsdp": lax.rem(me + 1, n)}, device_id_type=MESH,
        )

    load_og.wait()
    own(og_copy, start)

    for c in range(chunks):
        load_w(c).wait()
        own(w_copy(c), start)

    def send_acts(near):
        @pl.loop(1, n)
        def _(k):
            apart = jnp.abs(lax.rem(me + k, n) // 2 - z)
            pl.when((apart == 1) == near)(lambda: a_copy(k).start())

    def ag_store(s):
        return pltpu.make_async_copy(ag.at[s], ag_hbm.at[:, cols(s)], ag_sem.at[s])

    def use_weight(s):
        for c in range(chunks):
            part = slice(c * rows, (c + 1) * rows)
            vals[...] += jnp.dot(acts[s, :, part], w_all[s, c], preferred_element_type=F32)
            ag[s, :, part] = lax.dot_general(
                og_all[me], w_all[s, c], (((1,), (1,)), ((), ())), preferred_element_type=F32
            ).astype(BF16)
        ag_store(s).start()

    def use_acts(a, s):
        wgrad[...] += lax.dot_general(
            a, og_all[s], (((0,), (0,)), ((), ())), preferred_element_type=F32
        )

    vals[...] = jnp.zeros_like(vals)
    wgrad[...] = jnp.zeros_like(wgrad)

    @pl.loop(0, n)
    def _(s):
        load_acts(s).wait()

    use_weight(me)
    use_acts(acts[me], me)

    def gather(k):
        forward(og_copy, k, start, True)
        for c in range(chunks):
            forward(w_copy(c), k, start, True)

    def use_line(k):
        @pl.loop(0, 2)
        def _(j):
            zz = z + (1 - 2 * j) * k

            @pl.when((zz >= 0) & (zz < line))
            def _():
                use_weight(zz * 2 + y)

    def use_partner(k):
        @pl.loop(0, 2)
        def _(j):
            zz = z + (1 - 2 * j) * k

            @pl.when((zz >= 0) & (zz < line) & ((k > 0) | (j == 0)))
            def _():
                s = zz * 2 + 1 - y
                for c in range(chunks):
                    w_copy(c)(s, PARTNER).wait_recv()
                use_weight(s)

    gather(1)
    send_acts(False)

    @pl.loop(2, line)
    def _(k):
        gather(k)
        pl.when(k == 2)(lambda: send_acts(True))

    @pl.loop(0, line)
    def _(zz):
        og_copy(zz * 2 + 1 - y, PARTNER).wait_recv()

    @pl.loop(1, n)
    def _(k):
        s = lax.rem(me + n - k, n)
        a_arrived(s).wait_recv()
        use_acts(acts_t[s], s)

    for j in range(groups):
        part = slice(j * block, (j + 1) * block)
        for c in range(chunks):
            across = slice(c * rows, (c + 1) * rows)
            inner[j, across] = (
                w_all[me, c, :, part].astype(F32) - rate * wgrad[across, part]
            )

    def r_copy(k):
        d = lax.rem(rep + k, groups)
        return pltpu.make_async_remote_copy(
            src_ref=inner.at[d], dst_ref=rep_in.at[rep],
            send_sem=r_send.at[k], recv_sem=r_recv.at[rep],
            device_id={"rep": d}, device_id_type=MESH,
        )

    def r_arrived(k):
        d = lax.rem(rep + k, groups)
        return pltpu.make_async_remote_copy(
            src_ref=inner.at[d], dst_ref=rep_in.at[d],
            send_sem=r_send.at[k], recv_sem=r_recv.at[d],
            device_id={"rep": d}, device_id_type=MESH,
        )

    def o_copy(k):
        d = lax.rem(rep + k, groups)
        return pltpu.make_async_remote_copy(
            src_ref=outer_in.at[rep], dst_ref=outer_in.at[rep],
            send_sem=o_send.at[k], recv_sem=o_recv.at[rep],
            device_id={"rep": d}, device_id_type=MESH,
        )

    def o_arrived(k):
        d = lax.rem(rep + k, groups)
        return pltpu.make_async_remote_copy(
            src_ref=outer_in.at[d], dst_ref=outer_in.at[d],
            send_sem=o_send.at[k], recv_sem=o_recv.at[d],
            device_id={"rep": d}, device_id_type=MESH,
        )

    for k in range(1, groups):
        r_copy(k).start()
    rep_in[rep] = inner[rep]

    use_partner(0)

    @pl.loop(1, line - 1)
    def _(k):
        use_line(k)
        use_partner(k)

    for k in range(1, groups):
        r_arrived(k).wait_recv()
    load_anchor.wait()
    load_mom.wait()
    total = rep_in[0]
    for j in range(1, groups):
        total = total + rep_in[j]
    pseudo_grad = anchor[...] - total / groups
    mom_next = momentum_coef * mom[...] + pseudo_grad
    outer_in[rep] = (
        anchor[...] - outer_rate * (pseudo_grad + momentum_coef * mom_next)
    ).astype(BF16)
    for k in range(1, groups):
        o_copy(k).start()
    synced = jnp.full(mom_next.shape, plan[rep], jnp.int32) > 0
    new_mom_out[...] = jnp.where(synced, mom_next, mom[...])

    use_line(line - 1)
    use_partner(line - 1)
    values_out[...] = vals[...].astype(BF16)

    for k in range(1, groups):
        o_arrived(k).wait_recv()
    for j in range(groups):
        synced = jnp.full(inner.shape[1:], plan[j], jnp.int32) > 0
        new_w_out[:, j * block:(j + 1) * block] = jnp.where(
            synced, outer_in[j].astype(F32), inner[j]
        ).astype(BF16)

    own(og_copy, wait_send)
    for c in range(chunks):
        own(w_copy(c), wait_send)

    @pl.loop(1, line)
    def _(k):
        forward(og_copy, k, wait_send, False)
        for c in range(chunks):
            forward(w_copy(c), k, wait_send, False)

    @pl.loop(1, n)
    def _(k):
        a_copy(k).wait_send()

    for k in range(1, groups):
        r_copy(k).wait_send()
        o_copy(k).wait_send()

    @pl.loop(0, n)
    def _(s):
        ag_store(s).wait()


def local(n, groups, acts, out_grad, weights, anchor, momentum, plan):
    tokens, depth = acts.shape[1:]
    rows, kvw = weights.shape[1:]
    block = anchor.shape[1]
    rate = 1.0 / math.sqrt(tokens * n * depth)
    chunks = 2
    any_spec = pl.BlockSpec(memory_space=pl.ANY)
    vmem = pl.BlockSpec(memory_space=pltpu.VMEM)
    dma = pltpu.SemaphoreType.DMA
    values, act_grad, new_w, new_mom = pl.pallas_call(
        functools.partial(kernel, n, groups, chunks, rate),
        out_shape=(
            jax.ShapeDtypeStruct((tokens, kvw), BF16),
            jax.ShapeDtypeStruct((tokens, depth), BF16),
            jax.ShapeDtypeStruct((rows, kvw), BF16),
            jax.ShapeDtypeStruct((rows, block), F32),
        ),
        in_specs=[pl.BlockSpec(memory_space=pltpu.SMEM)] + [any_spec] * 5,
        out_specs=(vmem, any_spec, vmem, vmem),
        scratch_shapes=[
            pltpu.VMEM((n, tokens, rows), BF16),
            pltpu.VMEM((n, tokens, rows), BF16),
            pltpu.VMEM((n, tokens, kvw), BF16),
            pltpu.VMEM((n, chunks, rows // chunks, kvw), BF16),
            pltpu.VMEM((n, tokens, rows), BF16),
            pltpu.VMEM((tokens, kvw), F32),
            pltpu.VMEM((rows, kvw), F32),
            pltpu.VMEM((groups, rows, block), F32),
            pltpu.VMEM((groups, rows, block), F32),
            pltpu.VMEM((groups, rows, block), BF16),
            pltpu.VMEM((rows, block), F32),
            pltpu.VMEM((rows, block), F32),
            dma((n,)), dma((1,)), dma((chunks,)), dma((2,)), dma((n,)),
            dma((n, 3)), dma((n,)), dma((n, chunks, 3)), dma((n, chunks)), dma((n,)), dma((n,)),
            dma((groups,)), dma((groups,)), dma((groups,)), dma((groups,)),
        ],
        compiler_params=pltpu.CompilerParams(
            collective_id=0, has_side_effects=True, vmem_limit_bytes=56 * 2**20
        ),
        cost_estimate=pl.CostEstimate(
            flops=6 * tokens * depth * kvw, bytes_accessed=24 * 2**20, transcendentals=0
        ),
    )(plan, acts[0], out_grad[0], weights[0], anchor, momentum)
    return values[None], act_grad[None], new_w[None], new_mom


def solution(mesh):
    placed = (
        P("rep", "fsdp", None),
        P("rep", "fsdp", None),
        P("rep", "fsdp", None),
        P("fsdp", "rep"),
        P("fsdp", "rep"),
        P(),
    )
    return jax.shard_map(
        functools.partial(local, mesh.shape["fsdp"], mesh.shape["rep"]),
        mesh=mesh,
        in_specs=placed,
        out_specs=(
            P("rep", "fsdp", None),
            P("rep", "fsdp", None),
            P("rep", "fsdp", None),
            P("fsdp", "rep"),
        ),
        check_vma=False,
    )
```

```python
import functools
import math

import jax
import jax.numpy as jnp
from jax import lax
from jax.experimental import pallas as pl
from jax.experimental.pallas import tpu as pltpu
from jax.sharding import PartitionSpec as P

outer_rate = 0.7
momentum_coef = 0.9
MESH = pl.DeviceIdType.MESH
F32 = jnp.float32
BF16 = jnp.bfloat16
LEFT, RIGHT, PARTNER = 0, 1, 2


def kernel(
    n, groups, chunks, rate,
    plan, acts_hbm, og_hbm, w_hbm, anchor_hbm, mom_hbm,
    values_out, ag_hbm, new_w_out, new_mom_out,
    acts, acts_t, og_all, w_all, w_own, ag, vals, wgrad, inner, rep_in, outer_in, anchor, mom,
    acts_sem, og_sem, w_sem, state_sem, ag_sem,
    og_send, og_recv, w_send, w_recv, a_send, a_recv,
    r_send, r_recv, o_send, o_recv,
):
    me = lax.axis_index("fsdp")
    rep = lax.axis_index("rep")
    line = n // 2
    z = me // 2
    y = lax.rem(me, 2)
    width = acts.shape[2]
    rows = w_all.shape[2]
    block = anchor.shape[1]
    parts, span = acts_t.shape[0], acts_t.shape[3]

    def cols(s):
        return pl.ds(pl.multiple_of(s * width, width), width)

    def load_acts(s):
        return pltpu.make_async_copy(acts_hbm.at[:, cols(s)], acts.at[s], acts_sem.at[s])

    def load_w(c):
        return pltpu.make_async_copy(
            w_hbm.at[pl.ds(c * rows, rows)], w_all.at[me, c], w_sem.at[c]
        )

    load_og = pltpu.make_async_copy(og_hbm, og_all.at[me], og_sem.at[0])
    load_anchor = pltpu.make_async_copy(anchor_hbm, anchor, state_sem.at[0])
    load_mom = pltpu.make_async_copy(mom_hbm, mom, state_sem.at[1])
    load_og.start()
    for c in range(chunks):
        load_w(c).start()

    @pl.loop(0, n)
    def _(s):
        load_acts(s).start()

    def load_own(h):
        return pltpu.make_async_copy(
            w_hbm.at[pl.ds(h * span, span)], w_own.at[h], state_sem.at[2 + h]
        )

    for h in range(parts):
        load_own(h).start()
    load_anchor.start()
    load_mom.start()

    barrier = pltpu.get_barrier_semaphore()

    @pl.loop(1, n)
    def _(k):
        pl.semaphore_signal(
            barrier, inc=1, device_id={"fsdp": lax.rem(me + k, n)}, device_id_type=MESH
        )

    @pl.loop(1, groups)
    def _(k):
        pl.semaphore_signal(
            barrier, inc=1, device_id={"rep": lax.rem(rep + k, groups)}, device_id_type=MESH
        )

    pl.semaphore_wait(barrier, n - 1 + groups - 1)

    def target(way):
        return (jnp.maximum(me - 2, 0), jnp.minimum(me + 2, n - 1), me + 1 - 2 * y)[way]

    def og_copy(s, way):
        return pltpu.make_async_remote_copy(
            src_ref=og_all.at[s], dst_ref=og_all.at[s],
            send_sem=og_send.at[s, way], recv_sem=og_recv.at[s],
            device_id={"fsdp": target(way)}, device_id_type=MESH,
        )

    def w_copy(c):
        def make(s, way):
            return pltpu.make_async_remote_copy(
                src_ref=w_all.at[s, c], dst_ref=w_all.at[s, c],
                send_sem=w_send.at[s, c, way], recv_sem=w_recv.at[s, c],
                device_id={"fsdp": target(way)}, device_id_type=MESH,
            )
        return make

    def own(make, act):
        s = me
        pl.when(z > 0)(lambda: act(make(s, LEFT)))
        pl.when(z < line - 1)(lambda: act(make(s, RIGHT)))
        act(make(s, PARTNER))

    def forward(make, k, act, wait):
        @pl.when(z >= k)
        def _():
            s = me - 2 * k
            if wait:
                make(s, PARTNER).wait_recv()
            pl.when(z < line - 1)(lambda: act(make(s, RIGHT)))
            act(make(s, PARTNER))

        @pl.when(z + k < line)
        def _():
            s = me + 2 * k
            if wait:
                make(s, PARTNER).wait_recv()
            pl.when(z > 0)(lambda: act(make(s, LEFT)))
            act(make(s, PARTNER))

    def start(copy):
        copy.start()

    def wait_send(copy):
        copy.wait_send()

    def piece(s, h):
        return pl.ds(pl.multiple_of(s * width + h * span, span), span)

    def a_copy(k, h):
        d = lax.rem(me + k, n)
        return pltpu.make_async_remote_copy(
            src_ref=acts_hbm.at[:, piece(d, h)], dst_ref=acts_t.at[h, me],
            send_sem=a_send.at[k, h], recv_sem=a_recv.at[me, h],
            device_id={"fsdp": d}, device_id_type=MESH,
        )

    def a_arrived(s, h):
        return pltpu.make_async_remote_copy(
            src_ref=acts_hbm.at[:, piece(s, h)], dst_ref=acts_t.at[h, s],
            send_sem=a_send.at[0, h], recv_sem=a_recv.at[s, h],
            device_id={"fsdp": lax.rem(me + 1, n)}, device_id_type=MESH,
        )

    load_og.wait()
    own(og_copy, start)

    for c in range(chunks):
        load_w(c).wait()
        own(w_copy(c), start)

    def send_acts(first, last):
        for h in range(first, last):
            @pl.loop(1, n)
            def _(k):
                a_copy(k, h).start()

    def ag_store(s):
        return pltpu.make_async_copy(ag.at[s], ag_hbm.at[:, cols(s)], ag_sem.at[s])

    def use_weight(s):
        for c in range(chunks):
            part = slice(c * rows, (c + 1) * rows)
            vals[...] += jnp.dot(acts[s, :, part], w_all[s, c], preferred_element_type=F32)
            ag[s, :, part] = lax.dot_general(
                og_all[me], w_all[s, c], (((1,), (1,)), ((), ())), preferred_element_type=F32
            ).astype(BF16)
        ag_store(s).start()

    def use_acts(a, s, h):
        wgrad[h] += lax.dot_general(
            a, og_all[s], (((0,), (0,)), ((), ())), preferred_element_type=F32
        )

    vals[...] = jnp.zeros_like(vals)
    wgrad[...] = jnp.zeros_like(wgrad)

    @pl.loop(0, n)
    def _(s):
        load_acts(s).wait()

    use_weight(me)
    for h in range(parts):
        use_acts(acts[me, :, h * span:(h + 1) * span], me, h)

    def gather(k):
        forward(og_copy, k, start, True)
        for c in range(chunks):
            forward(w_copy(c), k, start, True)

    def use_line(k):
        @pl.loop(0, 2)
        def _(j):
            zz = z + (1 - 2 * j) * k

            @pl.when((zz >= 0) & (zz < line))
            def _():
                use_weight(zz * 2 + y)

    def use_partner(k):
        @pl.loop(0, 2)
        def _(j):
            zz = z + (1 - 2 * j) * k

            @pl.when((zz >= 0) & (zz < line) & ((k > 0) | (j == 0)))
            def _():
                s = zz * 2 + 1 - y
                for c in range(chunks):
                    w_copy(c)(s, PARTNER).wait_recv()
                use_weight(s)

    gather(1)
    send_acts(0, (parts + 1) // 2)

    @pl.loop(2, line)
    def _(k):
        gather(k)
        pl.when(k == 2)(lambda: send_acts((parts + 1) // 2, parts))

    @pl.loop(0, line)
    def _(zz):
        og_copy(zz * 2 + 1 - y, PARTNER).wait_recv()

    def r_copy(k, h):
        d = lax.rem(rep + k, groups)
        return pltpu.make_async_remote_copy(
            src_ref=inner.at[h, d], dst_ref=rep_in.at[h, rep],
            send_sem=r_send.at[k, h], recv_sem=r_recv.at[rep, h],
            device_id={"rep": d}, device_id_type=MESH,
        )

    def r_arrived(k, h):
        d = lax.rem(rep + k, groups)
        return pltpu.make_async_remote_copy(
            src_ref=inner.at[h, d], dst_ref=rep_in.at[h, d],
            send_sem=r_send.at[k, h], recv_sem=r_recv.at[d, h],
            device_id={"rep": d}, device_id_type=MESH,
        )

    def o_copy(k, h):
        d = lax.rem(rep + k, groups)
        return pltpu.make_async_remote_copy(
            src_ref=outer_in.at[h, rep], dst_ref=outer_in.at[h, rep],
            send_sem=o_send.at[k, h], recv_sem=o_recv.at[rep, h],
            device_id={"rep": d}, device_id_type=MESH,
        )

    def o_arrived(k, h):
        d = lax.rem(rep + k, groups)
        return pltpu.make_async_remote_copy(
            src_ref=outer_in.at[h, d], dst_ref=outer_in.at[h, d],
            send_sem=o_send.at[k, h], recv_sem=o_recv.at[d, h],
            device_id={"rep": d}, device_id_type=MESH,
        )

    def inner_step(h):
        @pl.loop(1, n)
        def _(k):
            s = lax.rem(me + n - k, n)
            a_arrived(s, h).wait_recv()
            use_acts(acts_t[h, s], s, h)

        for j in range(groups):
            part = slice(j * block, (j + 1) * block)
            inner[h, j] = w_own[h, :, part].astype(F32) - rate * wgrad[h, :, part]
        for k in range(1, groups):
            r_copy(k, h).start()
        rep_in[h, rep] = inner[h, rep]

    def outer_step(h):
        across = slice(h * span, (h + 1) * span)
        for k in range(1, groups):
            r_arrived(k, h).wait_recv()
        total = rep_in[h, 0]
        for j in range(1, groups):
            total = total + rep_in[h, j]
        pseudo_grad = anchor[across] - total / groups
        mom_next = momentum_coef * mom[across] + pseudo_grad
        outer_in[h, rep] = (
            anchor[across] - outer_rate * (pseudo_grad + momentum_coef * mom_next)
        ).astype(BF16)
        for k in range(1, groups):
            o_copy(k, h).start()
        synced = jnp.full(mom_next.shape, plan[rep], jnp.int32) > 0
        new_mom_out[across] = jnp.where(synced, mom_next, mom[across])

    def last_step(h):
        across = slice(h * span, (h + 1) * span)
        for k in range(1, groups):
            o_arrived(k, h).wait_recv()
        for j in range(groups):
            synced = jnp.full(inner.shape[2:], plan[j], jnp.int32) > 0
            new_w_out[across, j * block:(j + 1) * block] = jnp.where(
                synced, outer_in[h, j].astype(F32), inner[h, j]
            ).astype(BF16)

    load_anchor.wait()
    load_mom.wait()
    for c in range(parts):
        load_own(c).wait()
    inner_step(0)
    for h in range(1, parts):
        inner_step(h)
        outer_step(h - 1)
    use_partner(0)

    @pl.loop(1, line - 1)
    def _(k):
        use_line(k)
        use_partner(k)

    use_line(line - 1)
    outer_step(parts - 1)
    for h in range(parts - 1):
        last_step(h)
    use_partner(line - 1)
    values_out[...] = vals[...].astype(BF16)
    last_step(parts - 1)

    own(og_copy, wait_send)
    for c in range(chunks):
        own(w_copy(c), wait_send)

    @pl.loop(1, line)
    def _(k):
        forward(og_copy, k, wait_send, False)
        for c in range(chunks):
            forward(w_copy(c), k, wait_send, False)

    @pl.loop(1, n)
    def _(k):
        for h in range(parts):
            a_copy(k, h).wait_send()

    for k in range(1, groups):
        for h in range(parts):
            r_copy(k, h).wait_send()
            o_copy(k, h).wait_send()

    @pl.loop(0, n)
    def _(s):
        ag_store(s).wait()


def local(n, groups, acts, out_grad, weights, anchor, momentum, plan):
    tokens, depth = acts.shape[1:]
    rows, kvw = weights.shape[1:]
    block = anchor.shape[1]
    rate = 1.0 / math.sqrt(tokens * n * depth)
    parts = chunks = max(1, min(4, rows // 256))
    span = rows // parts
    any_spec = pl.BlockSpec(memory_space=pl.ANY)
    vmem = pl.BlockSpec(memory_space=pltpu.VMEM)
    dma = pltpu.SemaphoreType.DMA
    values, act_grad, new_w, new_mom = pl.pallas_call(
        functools.partial(kernel, n, groups, chunks, rate),
        out_shape=(
            jax.ShapeDtypeStruct((tokens, kvw), BF16),
            jax.ShapeDtypeStruct((tokens, depth), BF16),
            jax.ShapeDtypeStruct((rows, kvw), BF16),
            jax.ShapeDtypeStruct((rows, block), F32),
        ),
        in_specs=[pl.BlockSpec(memory_space=pltpu.SMEM)] + [any_spec] * 5,
        out_specs=(vmem, any_spec, vmem, vmem),
        scratch_shapes=[
            pltpu.VMEM((n, tokens, rows), BF16),
            pltpu.VMEM((parts, n, tokens, span), BF16),
            pltpu.VMEM((n, tokens, kvw), BF16),
            pltpu.VMEM((n, chunks, rows // chunks, kvw), BF16),
            pltpu.VMEM((parts, span, kvw), BF16),
            pltpu.VMEM((n, tokens, rows), BF16),
            pltpu.VMEM((tokens, kvw), F32),
            pltpu.VMEM((parts, span, kvw), F32),
            pltpu.VMEM((parts, groups, span, block), F32),
            pltpu.VMEM((parts, groups, span, block), F32),
            pltpu.VMEM((parts, groups, span, block), BF16),
            pltpu.VMEM((rows, block), F32),
            pltpu.VMEM((rows, block), F32),
            dma((n,)), dma((1,)), dma((chunks,)), dma((2 + parts,)), dma((n,)),
            dma((n, 3)), dma((n,)), dma((n, chunks, 3)), dma((n, chunks)),
            dma((n, parts)), dma((n, parts)),
            dma((groups, parts)), dma((groups, parts)), dma((groups, parts)), dma((groups, parts)),
        ],
        compiler_params=pltpu.CompilerParams(
            collective_id=0, has_side_effects=True, vmem_limit_bytes=56 * 2**20
        ),
        cost_estimate=pl.CostEstimate(
            flops=6 * tokens * depth * kvw, bytes_accessed=24 * 2**20, transcendentals=0
        ),
    )(plan, acts[0], out_grad[0], weights[0], anchor, momentum)
    return values[None], act_grad[None], new_w[None], new_mom


def solution(mesh):
    placed = (
        P("rep", "fsdp", None),
        P("rep", "fsdp", None),
        P("rep", "fsdp", None),
        P("fsdp", "rep"),
        P("fsdp", "rep"),
        P(),
    )
    return jax.shard_map(
        functools.partial(local, mesh.shape["fsdp"], mesh.shape["rep"]),
        mesh=mesh,
        in_specs=placed,
        out_specs=(
            P("rep", "fsdp", None),
            P("rep", "fsdp", None),
            P("rep", "fsdp", None),
            P("fsdp", "rep"),
        ),
        check_vma=False,
    )
```

```python
import functools
import math

import jax
import jax.numpy as jnp
from jax import lax
from jax.experimental import pallas as pl
from jax.experimental.pallas import tpu as pltpu
from jax.sharding import PartitionSpec as P

outer_rate = 0.7
momentum_coef = 0.9
MESH = pl.DeviceIdType.MESH
F32 = jnp.float32
BF16 = jnp.bfloat16
LEFT, RIGHT, PARTNER = 0, 1, 2


def kernel(
    n, groups, chunks, rate,
    plan, acts_hbm, og_hbm, w_hbm, anchor_hbm, mom_hbm,
    values_out, ag_hbm, new_w_out, new_mom_out,
    acts, acts_t, og_all, w_all, w_own, ag, vals, wgrad, inner, rep_in, outer_in, anchor, mom,
    acts_sem, og_sem, w_sem, state_sem, ag_sem,
    og_send, og_recv, w_send, w_recv, a_send, a_recv,
    r_send, r_recv, o_send, o_recv,
):
    me = lax.axis_index("fsdp")
    rep = lax.axis_index("rep")
    line = n // 2
    z = me // 2
    y = lax.rem(me, 2)
    width = acts.shape[2]
    rows = w_all.shape[2]
    block = anchor.shape[1]
    parts, span = acts_t.shape[0], acts_t.shape[3]

    def cols(s):
        return pl.ds(pl.multiple_of(s * width, width), width)

    def load_acts(s):
        return pltpu.make_async_copy(acts_hbm.at[:, cols(s)], acts.at[s], acts_sem.at[s])

    def load_w(c):
        return pltpu.make_async_copy(
            w_hbm.at[pl.ds(c * rows, rows)], w_all.at[me, c], w_sem.at[c]
        )

    load_og = pltpu.make_async_copy(og_hbm, og_all.at[me], og_sem.at[0])
    load_anchor = pltpu.make_async_copy(anchor_hbm, anchor, state_sem.at[0])
    load_mom = pltpu.make_async_copy(mom_hbm, mom, state_sem.at[1])
    load_og.start()
    for c in range(chunks):
        load_w(c).start()

    @pl.loop(0, n)
    def _(s):
        load_acts(s).start()

    def load_own(h):
        return pltpu.make_async_copy(
            w_hbm.at[pl.ds(h * span, span)], w_own.at[h], state_sem.at[2 + h]
        )

    for h in range(parts):
        load_own(h).start()
    load_anchor.start()
    load_mom.start()

    barrier = pltpu.get_barrier_semaphore()

    @pl.loop(1, n)
    def _(k):
        pl.semaphore_signal(
            barrier, inc=1, device_id={"fsdp": lax.rem(me + k, n)}, device_id_type=MESH
        )

    @pl.loop(1, groups)
    def _(k):
        pl.semaphore_signal(
            barrier, inc=1, device_id={"rep": lax.rem(rep + k, groups)}, device_id_type=MESH
        )

    pl.semaphore_wait(barrier, n - 1 + groups - 1)

    def target(way):
        return (jnp.maximum(me - 2, 0), jnp.minimum(me + 2, n - 1), me + 1 - 2 * y)[way]

    def og_copy(s, way):
        return pltpu.make_async_remote_copy(
            src_ref=og_all.at[s], dst_ref=og_all.at[s],
            send_sem=og_send.at[s, way], recv_sem=og_recv.at[s],
            device_id={"fsdp": target(way)}, device_id_type=MESH,
        )

    def w_copy(c):
        def make(s, way):
            return pltpu.make_async_remote_copy(
                src_ref=w_all.at[s, c], dst_ref=w_all.at[s, c],
                send_sem=w_send.at[s, c, way], recv_sem=w_recv.at[s, c],
                device_id={"fsdp": target(way)}, device_id_type=MESH,
            )
        return make

    def own(make, act):
        s = me
        pl.when(z > 0)(lambda: act(make(s, LEFT)))
        pl.when(z < line - 1)(lambda: act(make(s, RIGHT)))
        act(make(s, PARTNER))

    def forward(make, k, act, wait):
        @pl.when(z >= k)
        def _():
            s = me - 2 * k
            if wait:
                make(s, PARTNER).wait_recv()
            pl.when(z < line - 1)(lambda: act(make(s, RIGHT)))
            act(make(s, PARTNER))

        @pl.when(z + k < line)
        def _():
            s = me + 2 * k
            if wait:
                make(s, PARTNER).wait_recv()
            pl.when(z > 0)(lambda: act(make(s, LEFT)))
            act(make(s, PARTNER))

    def start(copy):
        copy.start()

    def wait_send(copy):
        copy.wait_send()

    def piece(s, h):
        return pl.ds(pl.multiple_of(s * width + h * span, span), span)

    def a_copy(k, h):
        d = lax.rem(me + k, n)
        return pltpu.make_async_remote_copy(
            src_ref=acts_hbm.at[:, piece(d, h)], dst_ref=acts_t.at[h, me],
            send_sem=a_send.at[k, h], recv_sem=a_recv.at[me, h],
            device_id={"fsdp": d}, device_id_type=MESH,
        )

    def a_arrived(s, h):
        return pltpu.make_async_remote_copy(
            src_ref=acts_hbm.at[:, piece(s, h)], dst_ref=acts_t.at[h, s],
            send_sem=a_send.at[0, h], recv_sem=a_recv.at[s, h],
            device_id={"fsdp": lax.rem(me + 1, n)}, device_id_type=MESH,
        )

    load_og.wait()
    own(og_copy, start)

    for c in range(chunks):
        load_w(c).wait()
        own(w_copy(c), start)

    def send_acts(first, last):
        for h in range(first, last):
            @pl.loop(1, n)
            def _(k):
                a_copy(k, h).start()

    def ag_store(s):
        return pltpu.make_async_copy(ag.at[s], ag_hbm.at[:, cols(s)], ag_sem.at[s])

    def use_weight(s):
        for c in range(chunks):
            part = slice(c * rows, (c + 1) * rows)
            vals[...] += jnp.dot(acts[s, :, part], w_all[s, c], preferred_element_type=F32)
            ag[s, :, part] = lax.dot_general(
                og_all[me], w_all[s, c], (((1,), (1,)), ((), ())), preferred_element_type=F32
            ).astype(BF16)
        ag_store(s).start()

    def use_acts(a, s, h):
        wgrad[h] += lax.dot_general(
            a, og_all[s], (((0,), (0,)), ((), ())), preferred_element_type=F32
        )

    vals[...] = jnp.zeros_like(vals)
    wgrad[...] = jnp.zeros_like(wgrad)

    @pl.loop(0, n)
    def _(s):
        load_acts(s).wait()

    use_weight(me)
    for h in range(parts):
        use_acts(acts[me, :, h * span:(h + 1) * span], me, h)

    def gather(k):
        forward(og_copy, k, start, True)
        for c in range(chunks):
            forward(w_copy(c), k, start, True)

    def use_line(k):
        @pl.loop(0, 2)
        def _(j):
            zz = z + (1 - 2 * j) * k

            @pl.when((zz >= 0) & (zz < line))
            def _():
                use_weight(zz * 2 + y)

    def use_partner(k):
        @pl.loop(0, 2)
        def _(j):
            zz = z + (1 - 2 * j) * k

            @pl.when((zz >= 0) & (zz < line) & ((k > 0) | (j == 0)))
            def _():
                s = zz * 2 + 1 - y
                for c in range(chunks):
                    w_copy(c)(s, PARTNER).wait_recv()
                use_weight(s)

    gather(1)
    send_acts(0, (parts + 1) // 2)
    use_partner(0)

    @pl.loop(2, line)
    def _(k):
        gather(k)
        pl.when(k == 2)(lambda: send_acts((parts + 1) // 2, parts))
        use_line(k - 1)
        use_partner(k - 1)

    @pl.loop(0, line)
    def _(zz):
        og_copy(zz * 2 + 1 - y, PARTNER).wait_recv()

    def r_copy(k, h):
        d = lax.rem(rep + k, groups)
        return pltpu.make_async_remote_copy(
            src_ref=inner.at[h, d], dst_ref=rep_in.at[h, rep],
            send_sem=r_send.at[k, h], recv_sem=r_recv.at[rep, h],
            device_id={"rep": d}, device_id_type=MESH,
        )

    def r_arrived(k, h):
        d = lax.rem(rep + k, groups)
        return pltpu.make_async_remote_copy(
            src_ref=inner.at[h, d], dst_ref=rep_in.at[h, d],
            send_sem=r_send.at[k, h], recv_sem=r_recv.at[d, h],
            device_id={"rep": d}, device_id_type=MESH,
        )

    def o_copy(k, h):
        d = lax.rem(rep + k, groups)
        return pltpu.make_async_remote_copy(
            src_ref=outer_in.at[h, rep], dst_ref=outer_in.at[h, rep],
            send_sem=o_send.at[k, h], recv_sem=o_recv.at[rep, h],
            device_id={"rep": d}, device_id_type=MESH,
        )

    def o_arrived(k, h):
        d = lax.rem(rep + k, groups)
        return pltpu.make_async_remote_copy(
            src_ref=outer_in.at[h, d], dst_ref=outer_in.at[h, d],
            send_sem=o_send.at[k, h], recv_sem=o_recv.at[d, h],
            device_id={"rep": d}, device_id_type=MESH,
        )

    def inner_step(h):
        @pl.loop(1, n)
        def _(k):
            s = lax.rem(me + n - k, n)
            a_arrived(s, h).wait_recv()
            use_acts(acts_t[h, s], s, h)

        for j in range(groups):
            part = slice(j * block, (j + 1) * block)
            inner[h, j] = w_own[h, :, part].astype(F32) - rate * wgrad[h, :, part]
        for k in range(1, groups):
            r_copy(k, h).start()
        rep_in[h, rep] = inner[h, rep]

    def outer_step(h):
        across = slice(h * span, (h + 1) * span)
        for k in range(1, groups):
            r_arrived(k, h).wait_recv()
        total = rep_in[h, 0]
        for j in range(1, groups):
            total = total + rep_in[h, j]
        pseudo_grad = anchor[across] - total / groups
        mom_next = momentum_coef * mom[across] + pseudo_grad
        outer_in[h, rep] = (
            anchor[across] - outer_rate * (pseudo_grad + momentum_coef * mom_next)
        ).astype(BF16)
        for k in range(1, groups):
            o_copy(k, h).start()
        synced = jnp.full(mom_next.shape, plan[rep], jnp.int32) > 0
        new_mom_out[across] = jnp.where(synced, mom_next, mom[across])

    def last_step(h):
        across = slice(h * span, (h + 1) * span)
        for k in range(1, groups):
            o_arrived(k, h).wait_recv()
        for j in range(groups):
            synced = jnp.full(inner.shape[2:], plan[j], jnp.int32) > 0
            new_w_out[across, j * block:(j + 1) * block] = jnp.where(
                synced, outer_in[h, j].astype(F32), inner[h, j]
            ).astype(BF16)

    load_anchor.wait()
    load_mom.wait()
    for c in range(parts):
        load_own(c).wait()
    inner_step(0)
    for h in range(1, parts):
        inner_step(h)
        outer_step(h - 1)
    use_line(line - 1)
    outer_step(parts - 1)
    for h in range(parts - 1):
        last_step(h)
    use_partner(line - 1)
    values_out[...] = vals[...].astype(BF16)
    last_step(parts - 1)

    own(og_copy, wait_send)
    for c in range(chunks):
        own(w_copy(c), wait_send)

    @pl.loop(1, line)
    def _(k):
        forward(og_copy, k, wait_send, False)
        for c in range(chunks):
            forward(w_copy(c), k, wait_send, False)

    @pl.loop(1, n)
    def _(k):
        for h in range(parts):
            a_copy(k, h).wait_send()

    for k in range(1, groups):
        for h in range(parts):
            r_copy(k, h).wait_send()
            o_copy(k, h).wait_send()

    @pl.loop(0, n)
    def _(s):
        ag_store(s).wait()


def local(n, groups, acts, out_grad, weights, anchor, momentum, plan):
    tokens, depth = acts.shape[1:]
    rows, kvw = weights.shape[1:]
    block = anchor.shape[1]
    rate = 1.0 / math.sqrt(tokens * n * depth)
    parts = chunks = max(1, min(4, rows // 256))
    span = rows // parts
    any_spec = pl.BlockSpec(memory_space=pl.ANY)
    hbm = pl.BlockSpec(memory_space=pltpu.HBM)
    held = (
        6 * n * tokens * rows + 2 * n * (tokens + rows) * kvw + 6 * tokens * kvw
        + 18 * rows * kvw + 12 * rows * block
    )
    vmem = pl.BlockSpec(memory_space=pltpu.VMEM)
    dma = pltpu.SemaphoreType.DMA
    values, act_grad, new_w, new_mom = pl.pallas_call(
        functools.partial(kernel, n, groups, chunks, rate),
        out_shape=(
            jax.ShapeDtypeStruct((tokens, kvw), BF16),
            jax.ShapeDtypeStruct((tokens, depth), BF16),
            jax.ShapeDtypeStruct((rows, kvw), BF16),
            jax.ShapeDtypeStruct((rows, block), F32),
        ),
        in_specs=[pl.BlockSpec(memory_space=pltpu.SMEM)] + [hbm] * 5,
        out_specs=(vmem, any_spec, vmem, vmem),
        scratch_shapes=[
            pltpu.VMEM((n, tokens, rows), BF16),
            pltpu.VMEM((parts, n, tokens, span), BF16),
            pltpu.VMEM((n, tokens, kvw), BF16),
            pltpu.VMEM((n, chunks, rows // chunks, kvw), BF16),
            pltpu.VMEM((parts, span, kvw), BF16),
            pltpu.VMEM((n, tokens, rows), BF16),
            pltpu.VMEM((tokens, kvw), F32),
            pltpu.VMEM((parts, span, kvw), F32),
            pltpu.VMEM((parts, groups, span, block), F32),
            pltpu.VMEM((parts, groups, span, block), F32),
            pltpu.VMEM((parts, groups, span, block), BF16),
            pltpu.VMEM((rows, block), F32),
            pltpu.VMEM((rows, block), F32),
            dma((n,)), dma((1,)), dma((chunks,)), dma((2 + parts,)), dma((n,)),
            dma((n, 3)), dma((n,)), dma((n, chunks, 3)), dma((n, chunks)),
            dma((n, parts)), dma((n, parts)),
            dma((groups, parts)), dma((groups, parts)), dma((groups, parts)), dma((groups, parts)),
        ],
        compiler_params=pltpu.CompilerParams(
            collective_id=0, has_side_effects=True, vmem_limit_bytes=held + 4 * 2**20
        ),
        cost_estimate=pl.CostEstimate(
            flops=6 * tokens * depth * kvw, bytes_accessed=24 * 2**20, transcendentals=0
        ),
    )(plan, acts[0], out_grad[0], weights[0], anchor, momentum)
    return values[None], act_grad[None], new_w[None], new_mom


def solution(mesh):
    placed = (
        P("rep", "fsdp", None),
        P("rep", "fsdp", None),
        P("rep", "fsdp", None),
        P("fsdp", "rep"),
        P("fsdp", "rep"),
        P(),
    )
    return jax.shard_map(
        functools.partial(local, mesh.shape["fsdp"], mesh.shape["rep"]),
        mesh=mesh,
        in_specs=placed,
        out_specs=(
            P("rep", "fsdp", None),
            P("rep", "fsdp", None),
            P("rep", "fsdp", None),
            P("fsdp", "rep"),
        ),
        check_vma=False,
    )
```

```python
import functools
import math

import jax
import jax.numpy as jnp
from jax import lax
from jax.experimental import pallas as pl
from jax.experimental.pallas import tpu as pltpu
from jax.sharding import PartitionSpec as P

outer_rate = 0.7
momentum_coef = 0.9
MESH = pl.DeviceIdType.MESH
F32 = jnp.float32
BF16 = jnp.bfloat16
LEFT, RIGHT, PARTNER = 0, 1, 2


def kernel(
    n, groups, chunks, rate,
    plan, acts_hbm, og_hbm, w_hbm, anchor_hbm, mom_hbm,
    values_out, ag_hbm, new_w_out, new_mom_out,
    acts, acts_t, og_all, w_all, w_own, ag, vals, wgrad, inner, rep_in, outer_in, anchor, mom,
    acts_sem, og_sem, w_sem, state_sem, ag_sem,
    og_send, og_recv, w_send, w_recv, a_send, a_recv,
    r_send, r_recv, o_send, o_recv,
):
    me = lax.axis_index("fsdp")
    rep = lax.axis_index("rep")
    line = n // 2
    z = me // 2
    y = lax.rem(me, 2)
    width = acts.shape[2]
    rows = w_all.shape[2]
    block = anchor.shape[1]
    parts, span = acts_t.shape[0], acts_t.shape[3]

    def cols(s):
        return pl.ds(pl.multiple_of(s * width, width), width)

    def load_acts(s):
        return pltpu.make_async_copy(acts_hbm.at[:, cols(s)], acts.at[s], acts_sem.at[s])

    def load_w(c):
        return pltpu.make_async_copy(
            w_hbm.at[pl.ds(c * rows, rows)], w_all.at[me, c], w_sem.at[c]
        )

    load_og = pltpu.make_async_copy(og_hbm, og_all.at[me], og_sem.at[0])
    load_anchor = pltpu.make_async_copy(anchor_hbm, anchor, state_sem.at[0])
    load_mom = pltpu.make_async_copy(mom_hbm, mom, state_sem.at[1])
    load_og.start()
    for c in range(chunks):
        load_w(c).start()

    @pl.loop(0, n)
    def _(s):
        load_acts(s).start()

    def load_own(h):
        return pltpu.make_async_copy(
            w_hbm.at[pl.ds(h * span, span)], w_own.at[h], state_sem.at[2 + h]
        )

    for h in range(parts):
        load_own(h).start()
    load_anchor.start()
    load_mom.start()

    barrier = pltpu.get_barrier_semaphore()

    @pl.loop(1, n)
    def _(k):
        pl.semaphore_signal(
            barrier, inc=1, device_id={"fsdp": lax.rem(me + k, n)}, device_id_type=MESH
        )

    @pl.loop(1, groups)
    def _(k):
        pl.semaphore_signal(
            barrier, inc=1, device_id={"rep": lax.rem(rep + k, groups)}, device_id_type=MESH
        )

    pl.semaphore_wait(barrier, n - 1 + groups - 1)

    def target(way):
        return (jnp.maximum(me - 2, 0), jnp.minimum(me + 2, n - 1), me + 1 - 2 * y)[way]

    def og_copy(s, way):
        return pltpu.make_async_remote_copy(
            src_ref=og_all.at[s], dst_ref=og_all.at[s],
            send_sem=og_send.at[s, way], recv_sem=og_recv.at[s],
            device_id={"fsdp": target(way)}, device_id_type=MESH,
        )

    def w_copy(c):
        def make(s, way):
            return pltpu.make_async_remote_copy(
                src_ref=w_all.at[s, c], dst_ref=w_all.at[s, c],
                send_sem=w_send.at[s, c, way], recv_sem=w_recv.at[s, c],
                device_id={"fsdp": target(way)}, device_id_type=MESH,
            )
        return make

    def own(make, act):
        s = me
        pl.when(z > 0)(lambda: act(make(s, LEFT)))
        pl.when(z < line - 1)(lambda: act(make(s, RIGHT)))
        act(make(s, PARTNER))

    def forward(make, k, act, wait):
        @pl.when(z >= k)
        def _():
            s = me - 2 * k
            if wait:
                make(s, PARTNER).wait_recv()
            pl.when(z < line - 1)(lambda: act(make(s, RIGHT)))
            act(make(s, PARTNER))

        @pl.when(z + k < line)
        def _():
            s = me + 2 * k
            if wait:
                make(s, PARTNER).wait_recv()
            pl.when(z > 0)(lambda: act(make(s, LEFT)))
            act(make(s, PARTNER))

    def start(copy):
        copy.start()

    def wait_send(copy):
        copy.wait_send()

    def piece(s, h):
        return pl.ds(pl.multiple_of(s * width + h * span, span), span)

    toward = 1 - 2 * (z // (line // 2))

    def a_copy(k, h):
        d = lax.rem(me + toward * k + n, n)
        return pltpu.make_async_remote_copy(
            src_ref=acts_hbm.at[:, piece(d, h)], dst_ref=acts_t.at[h, me],
            send_sem=a_send.at[k, h], recv_sem=a_recv.at[me, h],
            device_id={"fsdp": d}, device_id_type=MESH,
        )

    def a_arrived(s, h):
        return pltpu.make_async_remote_copy(
            src_ref=acts_hbm.at[:, piece(s, h)], dst_ref=acts_t.at[h, s],
            send_sem=a_send.at[0, h], recv_sem=a_recv.at[s, h],
            device_id={"fsdp": lax.rem(me + 1, n)}, device_id_type=MESH,
        )

    load_og.wait()
    own(og_copy, start)

    for c in range(chunks):
        load_w(c).wait()
        own(w_copy(c), start)

    def send_acts(first, last):
        for h in range(first, last):
            @pl.loop(1, n)
            def _(k):
                a_copy(n - k, h).start()

    def ag_store(s):
        return pltpu.make_async_copy(ag.at[s], ag_hbm.at[:, cols(s)], ag_sem.at[s])

    def use_weight(s):
        for c in range(chunks):
            part = slice(c * rows, (c + 1) * rows)
            vals[...] += jnp.dot(acts[s, :, part], w_all[s, c], preferred_element_type=F32)
            ag[s, :, part] = lax.dot_general(
                og_all[me], w_all[s, c], (((1,), (1,)), ((), ())), preferred_element_type=F32
            ).astype(BF16)
        ag_store(s).start()

    def use_acts(a, s, h):
        wgrad[h] += lax.dot_general(
            a, og_all[s], (((0,), (0,)), ((), ())), preferred_element_type=F32
        )

    vals[...] = jnp.zeros_like(vals)
    wgrad[...] = jnp.zeros_like(wgrad)

    @pl.loop(0, n)
    def _(s):
        load_acts(s).wait()

    use_weight(me)
    for h in range(parts):
        use_acts(acts[me, :, h * span:(h + 1) * span], me, h)

    def gather(k):
        forward(og_copy, k, start, True)
        for c in range(chunks):
            forward(w_copy(c), k, start, True)

    def use_line(k):
        @pl.loop(0, 2)
        def _(j):
            zz = z + (1 - 2 * j) * k

            @pl.when((zz >= 0) & (zz < line))
            def _():
                use_weight(zz * 2 + y)

    def use_partner(k):
        @pl.loop(0, 2)
        def _(j):
            zz = z + (1 - 2 * j) * k

            @pl.when((zz >= 0) & (zz < line) & ((k > 0) | (j == 0)))
            def _():
                s = zz * 2 + 1 - y
                for c in range(chunks):
                    w_copy(c)(s, PARTNER).wait_recv()
                use_weight(s)

    gather(1)
    send_acts(0, (parts + 1) // 2)

    @pl.loop(2, line)
    def _(k):
        gather(k)
        pl.when(k == 2)(lambda: send_acts((parts + 1) // 2, parts))

        @pl.when(k == 2)
        def _():
            use_partner(0)
            use_line(1)

    @pl.loop(0, line)
    def _(zz):
        og_copy(zz * 2 + 1 - y, PARTNER).wait_recv()

    def r_copy(k, h):
        d = lax.rem(rep + k, groups)
        return pltpu.make_async_remote_copy(
            src_ref=inner.at[h, d], dst_ref=rep_in.at[h, rep],
            send_sem=r_send.at[k, h], recv_sem=r_recv.at[rep, h],
            device_id={"rep": d}, device_id_type=MESH,
        )

    def r_arrived(k, h):
        d = lax.rem(rep + k, groups)
        return pltpu.make_async_remote_copy(
            src_ref=inner.at[h, d], dst_ref=rep_in.at[h, d],
            send_sem=r_send.at[k, h], recv_sem=r_recv.at[d, h],
            device_id={"rep": d}, device_id_type=MESH,
        )

    def o_copy(k, h):
        d = lax.rem(rep + k, groups)
        return pltpu.make_async_remote_copy(
            src_ref=outer_in.at[h, rep], dst_ref=outer_in.at[h, rep],
            send_sem=o_send.at[k, h], recv_sem=o_recv.at[rep, h],
            device_id={"rep": d}, device_id_type=MESH,
        )

    def o_arrived(k, h):
        d = lax.rem(rep + k, groups)
        return pltpu.make_async_remote_copy(
            src_ref=outer_in.at[h, d], dst_ref=outer_in.at[h, d],
            send_sem=o_send.at[k, h], recv_sem=o_recv.at[d, h],
            device_id={"rep": d}, device_id_type=MESH,
        )

    def inner_step(h):
        @pl.loop(1, n)
        def _(k):
            s = lax.rem(me + n - k, n)
            a_arrived(s, h).wait_recv()
            use_acts(acts_t[h, s], s, h)

        for j in range(groups):
            part = slice(j * block, (j + 1) * block)
            inner[h, j] = w_own[h, :, part].astype(F32) - rate * wgrad[h, :, part]
        for k in range(1, groups):
            r_copy(k, h).start()
        rep_in[h, rep] = inner[h, rep]

    def outer_step(h):
        across = slice(h * span, (h + 1) * span)
        for k in range(1, groups):
            r_arrived(k, h).wait_recv()
        total = rep_in[h, 0]
        for j in range(1, groups):
            total = total + rep_in[h, j]
        pseudo_grad = anchor[across] - total / groups
        mom_next = momentum_coef * mom[across] + pseudo_grad
        outer_in[h, rep] = (
            anchor[across] - outer_rate * (pseudo_grad + momentum_coef * mom_next)
        ).astype(BF16)
        for k in range(1, groups):
            o_copy(k, h).start()
        synced = jnp.full(mom_next.shape, plan[rep], jnp.int32) > 0
        new_mom_out[across] = jnp.where(synced, mom_next, mom[across])

    def last_step(h):
        across = slice(h * span, (h + 1) * span)
        for k in range(1, groups):
            o_arrived(k, h).wait_recv()
        for j in range(groups):
            synced = jnp.full(inner.shape[2:], plan[j], jnp.int32) > 0
            new_w_out[across, j * block:(j + 1) * block] = jnp.where(
                synced, outer_in[h, j].astype(F32), inner[h, j]
            ).astype(BF16)

    load_anchor.wait()
    load_mom.wait()
    for c in range(parts):
        load_own(c).wait()
    inner_step(0)
    for h in range(1, parts):
        inner_step(h)
        outer_step(h - 1)
        if h == 1:
            use_partner(1)
    if parts == 1:
        use_partner(1)

    @pl.loop(2, line - 1)
    def _(k):
        use_line(k)
        use_partner(k)

    use_line(line - 1)
    outer_step(parts - 1)
    for h in range(parts - 1):
        last_step(h)
    use_partner(line - 1)
    values_out[...] = vals[...].astype(BF16)
    last_step(parts - 1)

    own(og_copy, wait_send)
    for c in range(chunks):
        own(w_copy(c), wait_send)

    @pl.loop(1, line)
    def _(k):
        forward(og_copy, k, wait_send, False)
        for c in range(chunks):
            forward(w_copy(c), k, wait_send, False)

    @pl.loop(1, n)
    def _(k):
        for h in range(parts):
            a_copy(k, h).wait_send()

    for k in range(1, groups):
        for h in range(parts):
            r_copy(k, h).wait_send()
            o_copy(k, h).wait_send()

    @pl.loop(0, n)
    def _(s):
        ag_store(s).wait()


def local(n, groups, acts, out_grad, weights, anchor, momentum, plan):
    tokens, depth = acts.shape[1:]
    rows, kvw = weights.shape[1:]
    block = anchor.shape[1]
    rate = 1.0 / math.sqrt(tokens * n * depth)
    parts = chunks = max(1, min(4, rows // 256))
    span = rows // parts
    any_spec = pl.BlockSpec(memory_space=pl.ANY)
    vmem = pl.BlockSpec(memory_space=pltpu.VMEM)
    dma = pltpu.SemaphoreType.DMA
    values, act_grad, new_w, new_mom = pl.pallas_call(
        functools.partial(kernel, n, groups, chunks, rate),
        out_shape=(
            jax.ShapeDtypeStruct((tokens, kvw), BF16),
            jax.ShapeDtypeStruct((tokens, depth), BF16),
            jax.ShapeDtypeStruct((rows, kvw), BF16),
            jax.ShapeDtypeStruct((rows, block), F32),
        ),
        in_specs=[pl.BlockSpec(memory_space=pltpu.SMEM)] + [any_spec] * 5,
        out_specs=(vmem, any_spec, vmem, vmem),
        scratch_shapes=[
            pltpu.VMEM((n, tokens, rows), BF16),
            pltpu.VMEM((parts, n, tokens, span), BF16),
            pltpu.VMEM((n, tokens, kvw), BF16),
            pltpu.VMEM((n, chunks, rows // chunks, kvw), BF16),
            pltpu.VMEM((parts, span, kvw), BF16),
            pltpu.VMEM((n, tokens, rows), BF16),
            pltpu.VMEM((tokens, kvw), F32),
            pltpu.VMEM((parts, span, kvw), F32),
            pltpu.VMEM((parts, groups, span, block), F32),
            pltpu.VMEM((parts, groups, span, block), F32),
            pltpu.VMEM((parts, groups, span, block), BF16),
            pltpu.VMEM((rows, block), F32),
            pltpu.VMEM((rows, block), F32),
            dma((n,)), dma((1,)), dma((chunks,)), dma((2 + parts,)), dma((n,)),
            dma((n, 3)), dma((n,)), dma((n, chunks, 3)), dma((n, chunks)),
            dma((n, parts)), dma((n, parts)),
            dma((groups, parts)), dma((groups, parts)), dma((groups, parts)), dma((groups, parts)),
        ],
        compiler_params=pltpu.CompilerParams(
            collective_id=0, has_side_effects=True, vmem_limit_bytes=56 * 2**20
        ),
        cost_estimate=pl.CostEstimate(
            flops=6 * tokens * depth * kvw, bytes_accessed=24 * 2**20, transcendentals=0
        ),
    )(plan, acts[0], out_grad[0], weights[0], anchor, momentum)
    return values[None], act_grad[None], new_w[None], new_mom


def solution(mesh):
    placed = (
        P("rep", "fsdp", None),
        P("rep", "fsdp", None),
        P("rep", "fsdp", None),
        P("fsdp", "rep"),
        P("fsdp", "rep"),
        P(),
    )
    return jax.shard_map(
        functools.partial(local, mesh.shape["fsdp"], mesh.shape["rep"]),
        mesh=mesh,
        in_specs=placed,
        out_specs=(
            P("rep", "fsdp", None),
            P("rep", "fsdp", None),
            P("rep", "fsdp", None),
            P("fsdp", "rep"),
        ),
        check_vma=False,
    )
```

```python
import functools
import math

import jax
import jax.numpy as jnp
from jax import lax
from jax.experimental import pallas as pl
from jax.experimental.pallas import tpu as pltpu
from jax.sharding import PartitionSpec as P

outer_rate = 0.7
momentum_coef = 0.9
MESH = pl.DeviceIdType.MESH
F32 = jnp.float32
BF16 = jnp.bfloat16
LEFT, RIGHT, PARTNER = 0, 1, 2


def kernel(
    n, groups, chunks, rate,
    plan, acts_hbm, og_hbm, w_hbm, anchor_hbm, mom_hbm,
    values_out, ag_hbm, new_w_out, new_mom_out,
    acts, acts_t, og_all, w_all, w_own, ag, vals, wgrad, inner, rep_in, outer_in, anchor, mom,
    acts_sem, og_sem, w_sem, state_sem, ag_sem,
    og_send, og_recv, w_send, w_recv, a_send, a_recv,
    r_send, r_recv, o_send, o_recv,
):
    me = lax.axis_index("fsdp")
    rep = lax.axis_index("rep")
    line = n // 2
    z = me // 2
    y = lax.rem(me, 2)
    width = acts.shape[2]
    rows = w_all.shape[2]
    block = anchor.shape[1]
    parts, span = acts_t.shape[0], acts_t.shape[3]

    def cols(s):
        return pl.ds(pl.multiple_of(s * width, width), width)

    def load_acts(s):
        return pltpu.make_async_copy(acts_hbm.at[:, cols(s)], acts.at[s], acts_sem.at[s])

    def load_w(c):
        return pltpu.make_async_copy(
            w_hbm.at[pl.ds(c * rows, rows)], w_all.at[me, c], w_sem.at[c]
        )

    load_og = pltpu.make_async_copy(og_hbm, og_all.at[me], og_sem.at[0])
    load_anchor = pltpu.make_async_copy(anchor_hbm, anchor, state_sem.at[0])
    load_mom = pltpu.make_async_copy(mom_hbm, mom, state_sem.at[1])
    load_og.start()
    for c in range(chunks):
        load_w(c).start()

    @pl.loop(0, n)
    def _(s):
        load_acts(s).start()

    def load_own(h):
        return pltpu.make_async_copy(
            w_hbm.at[pl.ds(h * span, span)], w_own.at[h], state_sem.at[2 + h]
        )

    for h in range(parts):
        load_own(h).start()
    load_anchor.start()
    load_mom.start()

    barrier = pltpu.get_barrier_semaphore()

    @pl.loop(1, n)
    def _(k):
        pl.semaphore_signal(
            barrier, inc=1, device_id={"fsdp": lax.rem(me + k, n)}, device_id_type=MESH
        )

    @pl.loop(1, groups)
    def _(k):
        pl.semaphore_signal(
            barrier, inc=1, device_id={"rep": lax.rem(rep + k, groups)}, device_id_type=MESH
        )

    pl.semaphore_wait(barrier, n - 1 + groups - 1)

    def target(way):
        return (jnp.maximum(me - 2, 0), jnp.minimum(me + 2, n - 1), me + 1 - 2 * y)[way]

    def og_copy(s, way):
        return pltpu.make_async_remote_copy(
            src_ref=og_all.at[s], dst_ref=og_all.at[s],
            send_sem=og_send.at[s, way], recv_sem=og_recv.at[s],
            device_id={"fsdp": target(way)}, device_id_type=MESH,
        )

    def w_copy(c):
        def make(s, way):
            return pltpu.make_async_remote_copy(
                src_ref=w_all.at[s, c], dst_ref=w_all.at[s, c],
                send_sem=w_send.at[s, c, way], recv_sem=w_recv.at[s, c],
                device_id={"fsdp": target(way)}, device_id_type=MESH,
            )
        return make

    def own(make, act):
        s = me
        pl.when(z > 0)(lambda: act(make(s, LEFT)))
        pl.when(z < line - 1)(lambda: act(make(s, RIGHT)))
        act(make(s, PARTNER))

    def forward(make, k, act, wait):
        @pl.when(z >= k)
        def _():
            s = me - 2 * k
            if wait:
                make(s, PARTNER).wait_recv()
            pl.when(z < line - 1)(lambda: act(make(s, RIGHT)))
            act(make(s, PARTNER))

        @pl.when(z + k < line)
        def _():
            s = me + 2 * k
            if wait:
                make(s, PARTNER).wait_recv()
            pl.when(z > 0)(lambda: act(make(s, LEFT)))
            act(make(s, PARTNER))

    def start(copy):
        copy.start()

    def wait_send(copy):
        copy.wait_send()

    def piece(s, h):
        return pl.ds(pl.multiple_of(s * width + h * span, span), span)

    toward = 1 - 2 * (z // (line // 2))

    def a_copy(k, h):
        d = lax.rem(me + toward * k + n, n)
        return pltpu.make_async_remote_copy(
            src_ref=acts_hbm.at[:, piece(d, h)], dst_ref=acts_t.at[h, me],
            send_sem=a_send.at[k, h], recv_sem=a_recv.at[me, h],
            device_id={"fsdp": d}, device_id_type=MESH,
        )

    def a_arrived(s, h):
        return pltpu.make_async_remote_copy(
            src_ref=acts_hbm.at[:, piece(s, h)], dst_ref=acts_t.at[h, s],
            send_sem=a_send.at[0, h], recv_sem=a_recv.at[s, h],
            device_id={"fsdp": lax.rem(me + 1, n)}, device_id_type=MESH,
        )

    load_og.wait()
    own(og_copy, start)

    for c in range(chunks):
        load_w(c).wait()
        own(w_copy(c), start)

    def send_acts(h):
        @pl.loop(1, n)
        def _(k):
            a_copy(n - k, h).start()

    def ag_store(s):
        return pltpu.make_async_copy(ag.at[s], ag_hbm.at[:, cols(s)], ag_sem.at[s])

    def use_weight(s):
        for c in range(chunks):
            part = slice(c * rows, (c + 1) * rows)
            vals[...] += jnp.dot(acts[s, :, part], w_all[s, c], preferred_element_type=F32)
            ag[s, :, part] = lax.dot_general(
                og_all[me], w_all[s, c], (((1,), (1,)), ((), ())), preferred_element_type=F32
            ).astype(BF16)
        ag_store(s).start()

    def use_acts(a, s, h):
        wgrad[h] += lax.dot_general(
            a, og_all[s], (((0,), (0,)), ((), ())), preferred_element_type=F32
        )

    vals[...] = jnp.zeros_like(vals)
    wgrad[...] = jnp.zeros_like(wgrad)

    @pl.loop(0, n)
    def _(s):
        load_acts(s).wait()

    use_weight(me)
    for h in range(parts):
        use_acts(acts[me, :, h * span:(h + 1) * span], me, h)

    def gather(k):
        forward(og_copy, k, start, True)
        for c in range(chunks):
            forward(w_copy(c), k, start, True)

    def use_line(k):
        @pl.loop(0, 2)
        def _(j):
            zz = z + (1 - 2 * j) * k

            @pl.when((zz >= 0) & (zz < line))
            def _():
                use_weight(zz * 2 + y)

    def use_partner(k):
        @pl.loop(0, 2)
        def _(j):
            zz = z + (1 - 2 * j) * k

            @pl.when((zz >= 0) & (zz < line) & ((k > 0) | (j == 0)))
            def _():
                s = zz * 2 + 1 - y
                for c in range(chunks):
                    w_copy(c)(s, PARTNER).wait_recv()
                use_weight(s)

    def r_copy(k, h):
        d = lax.rem(rep + k, groups)
        return pltpu.make_async_remote_copy(
            src_ref=inner.at[h, d], dst_ref=rep_in.at[h, rep],
            send_sem=r_send.at[k, h], recv_sem=r_recv.at[rep, h],
            device_id={"rep": d}, device_id_type=MESH,
        )

    def r_arrived(k, h):
        d = lax.rem(rep + k, groups)
        return pltpu.make_async_remote_copy(
            src_ref=inner.at[h, d], dst_ref=rep_in.at[h, d],
            send_sem=r_send.at[k, h], recv_sem=r_recv.at[d, h],
            device_id={"rep": d}, device_id_type=MESH,
        )

    def o_copy(k, h):
        d = lax.rem(rep + k, groups)
        return pltpu.make_async_remote_copy(
            src_ref=outer_in.at[h, rep], dst_ref=outer_in.at[h, rep],
            send_sem=o_send.at[k, h], recv_sem=o_recv.at[rep, h],
            device_id={"rep": d}, device_id_type=MESH,
        )

    def o_arrived(k, h):
        d = lax.rem(rep + k, groups)
        return pltpu.make_async_remote_copy(
            src_ref=outer_in.at[h, d], dst_ref=outer_in.at[h, d],
            send_sem=o_send.at[k, h], recv_sem=o_recv.at[d, h],
            device_id={"rep": d}, device_id_type=MESH,
        )

    def inner_step(h):
        @pl.loop(1, n)
        def _(k):
            s = lax.rem(me + n - k, n)
            a_arrived(s, h).wait_recv()
            use_acts(acts_t[h, s], s, h)

        for j in range(groups):
            part = slice(j * block, (j + 1) * block)
            inner[h, j] = w_own[h, :, part].astype(F32) - rate * wgrad[h, :, part]
        for k in range(1, groups):
            r_copy(k, h).start()
        rep_in[h, rep] = inner[h, rep]

    def outer_step(h):
        across = slice(h * span, (h + 1) * span)
        for k in range(1, groups):
            r_arrived(k, h).wait_recv()
        total = rep_in[h, 0]
        for j in range(1, groups):
            total = total + rep_in[h, j]
        pseudo_grad = anchor[across] - total / groups
        mom_next = momentum_coef * mom[across] + pseudo_grad
        outer_in[h, rep] = (
            anchor[across] - outer_rate * (pseudo_grad + momentum_coef * mom_next)
        ).astype(BF16)
        for k in range(1, groups):
            o_copy(k, h).start()
        synced = jnp.full(mom_next.shape, plan[rep], jnp.int32) > 0
        new_mom_out[across] = jnp.where(synced, mom_next, mom[across])

    def last_step(h):
        across = slice(h * span, (h + 1) * span)
        for k in range(1, groups):
            o_arrived(k, h).wait_recv()
        for j in range(groups):
            synced = jnp.full(inner.shape[2:], plan[j], jnp.int32) > 0
            new_w_out[across, j * block:(j + 1) * block] = jnp.where(
                synced, outer_in[h, j].astype(F32), inner[h, j]
            ).astype(BF16)

    load_anchor.wait()
    load_mom.wait()
    for h in range(parts):
        load_own(h).wait()

    gather(1)
    send_acts(0)

    @pl.loop(2, line - 1)
    def _(k):
        gather(k)

    if parts > 1:
        send_acts(1)
    use_line(1)
    use_partner(0)

    forward(og_copy, line - 1, start, True)

    @pl.loop(0, line)
    def _(zz):
        og_copy(zz * 2 + 1 - y, PARTNER).wait_recv()

    for h in range(parts):
        inner_step(h)
        if h + 2 < parts:
            send_acts(h + 2)
        if h == 0:
            for c in range(chunks):
                forward(w_copy(c), line - 1, start, True)
        if h > 0:
            outer_step(h - 1)
        if h == min(1, parts - 1):
            use_partner(1)

    @pl.loop(2, line - 1)
    def _(k):
        use_line(k)
        use_partner(k)

    use_line(line - 1)
    outer_step(parts - 1)
    for h in range(parts - 1):
        last_step(h)
    use_partner(line - 1)
    values_out[...] = vals[...].astype(BF16)
    last_step(parts - 1)

    own(og_copy, wait_send)
    for c in range(chunks):
        own(w_copy(c), wait_send)

    @pl.loop(1, line)
    def _(k):
        forward(og_copy, k, wait_send, False)
        for c in range(chunks):
            forward(w_copy(c), k, wait_send, False)

    @pl.loop(1, n)
    def _(k):
        for h in range(parts):
            a_copy(k, h).wait_send()

    for k in range(1, groups):
        for h in range(parts):
            r_copy(k, h).wait_send()
            o_copy(k, h).wait_send()

    @pl.loop(0, n)
    def _(s):
        ag_store(s).wait()


def local(n, groups, acts, out_grad, weights, anchor, momentum, plan):
    tokens, depth = acts.shape[1:]
    rows, kvw = weights.shape[1:]
    block = anchor.shape[1]
    rate = 1.0 / math.sqrt(tokens * n * depth)
    parts = chunks = max(1, min(4, rows // 256))
    span = rows // parts
    any_spec = pl.BlockSpec(memory_space=pl.ANY)
    vmem = pl.BlockSpec(memory_space=pltpu.VMEM)
    dma = pltpu.SemaphoreType.DMA
    values, act_grad, new_w, new_mom = pl.pallas_call(
        functools.partial(kernel, n, groups, chunks, rate),
        out_shape=(
            jax.ShapeDtypeStruct((tokens, kvw), BF16),
            jax.ShapeDtypeStruct((tokens, depth), BF16),
            jax.ShapeDtypeStruct((rows, kvw), BF16),
            jax.ShapeDtypeStruct((rows, block), F32),
        ),
        in_specs=[pl.BlockSpec(memory_space=pltpu.SMEM)] + [any_spec] * 5,
        out_specs=(vmem, any_spec, vmem, vmem),
        scratch_shapes=[
            pltpu.VMEM((n, tokens, rows), BF16),
            pltpu.VMEM((parts, n, tokens, span), BF16),
            pltpu.VMEM((n, tokens, kvw), BF16),
            pltpu.VMEM((n, chunks, rows // chunks, kvw), BF16),
            pltpu.VMEM((parts, span, kvw), BF16),
            pltpu.VMEM((n, tokens, rows), BF16),
            pltpu.VMEM((tokens, kvw), F32),
            pltpu.VMEM((parts, span, kvw), F32),
            pltpu.VMEM((parts, groups, span, block), F32),
            pltpu.VMEM((parts, groups, span, block), F32),
            pltpu.VMEM((parts, groups, span, block), BF16),
            pltpu.VMEM((rows, block), F32),
            pltpu.VMEM((rows, block), F32),
            dma((n,)), dma((1,)), dma((chunks,)), dma((2 + parts,)), dma((n,)),
            dma((n, 3)), dma((n,)), dma((n, chunks, 3)), dma((n, chunks)),
            dma((n, parts)), dma((n, parts)),
            dma((groups, parts)), dma((groups, parts)), dma((groups, parts)), dma((groups, parts)),
        ],
        compiler_params=pltpu.CompilerParams(
            collective_id=0, has_side_effects=True, vmem_limit_bytes=56 * 2**20
        ),
        cost_estimate=pl.CostEstimate(
            flops=6 * tokens * depth * kvw, bytes_accessed=24 * 2**20, transcendentals=0
        ),
    )(plan, acts[0], out_grad[0], weights[0], anchor, momentum)
    return values[None], act_grad[None], new_w[None], new_mom


def solution(mesh):
    placed = (
        P("rep", "fsdp", None),
        P("rep", "fsdp", None),
        P("rep", "fsdp", None),
        P("fsdp", "rep"),
        P("fsdp", "rep"),
        P(),
    )
    return jax.shard_map(
        functools.partial(local, mesh.shape["fsdp"], mesh.shape["rep"]),
        mesh=mesh,
        in_specs=placed,
        out_specs=(
            P("rep", "fsdp", None),
            P("rep", "fsdp", None),
            P("rep", "fsdp", None),
            P("fsdp", "rep"),
        ),
        check_vma=False,
    )
```

```python
import functools
import math

import jax
import jax.numpy as jnp
from jax import lax
from jax.experimental import pallas as pl
from jax.experimental.pallas import tpu as pltpu
from jax.sharding import PartitionSpec as P

outer_rate = 0.7
momentum_coef = 0.9
MESH = pl.DeviceIdType.MESH
F32 = jnp.float32
BF16 = jnp.bfloat16
LEFT, RIGHT, PARTNER = 0, 1, 2


def kernel(
    n, groups, chunks, rate,
    plan, acts_hbm, og_hbm, w_hbm, anchor_hbm, mom_hbm,
    values_out, ag_hbm, new_w_out, new_mom_out,
    acts, acts_t, og_all, w_all, w_own, ag, vals, wgrad, inner, rep_in, outer_in, anchor, mom,
    acts_sem, og_sem, w_sem, state_sem, ag_sem,
    og_send, og_recv, w_send, w_recv, a_send, a_recv,
    r_send, r_recv, o_send, o_recv,
):
    me = lax.axis_index("fsdp")
    rep = lax.axis_index("rep")
    line = n // 2
    z = me // 2
    y = lax.rem(me, 2)
    width = acts.shape[2]
    rows = w_all.shape[2]
    block = anchor.shape[1]
    parts, span = acts_t.shape[0], acts_t.shape[3]

    def cols(s):
        return pl.ds(pl.multiple_of(s * width, width), width)

    def load_acts(s):
        return pltpu.make_async_copy(acts_hbm.at[:, cols(s)], acts.at[s], acts_sem.at[s])

    def load_w(c):
        return pltpu.make_async_copy(
            w_hbm.at[pl.ds(c * rows, rows)], w_all.at[me, c], w_sem.at[c]
        )

    load_og = pltpu.make_async_copy(og_hbm, og_all.at[me], og_sem.at[0])
    load_anchor = pltpu.make_async_copy(anchor_hbm, anchor, state_sem.at[0])
    load_mom = pltpu.make_async_copy(mom_hbm, mom, state_sem.at[1])
    load_og.start()
    for c in range(chunks):
        load_w(c).start()

    @pl.loop(0, n)
    def _(s):
        load_acts(s).start()

    def load_own(h):
        return pltpu.make_async_copy(
            w_hbm.at[pl.ds(h * span, span)], w_own.at[h], state_sem.at[2 + h]
        )

    for h in range(parts):
        load_own(h).start()
    load_anchor.start()
    load_mom.start()

    barrier = pltpu.get_barrier_semaphore()

    @pl.loop(1, n)
    def _(k):
        pl.semaphore_signal(
            barrier, inc=1, device_id={"fsdp": lax.rem(me + k, n)}, device_id_type=MESH
        )

    @pl.loop(1, groups)
    def _(k):
        pl.semaphore_signal(
            barrier, inc=1, device_id={"rep": lax.rem(rep + k, groups)}, device_id_type=MESH
        )

    pl.semaphore_wait(barrier, n - 1 + groups - 1)

    def target(way):
        return (jnp.maximum(me - 2, 0), jnp.minimum(me + 2, n - 1), me + 1 - 2 * y)[way]

    def og_copy(s, way):
        return pltpu.make_async_remote_copy(
            src_ref=og_all.at[s], dst_ref=og_all.at[s],
            send_sem=og_send.at[s, way], recv_sem=og_recv.at[s],
            device_id={"fsdp": target(way)}, device_id_type=MESH,
        )

    def w_copy(c):
        def make(s, way):
            return pltpu.make_async_remote_copy(
                src_ref=w_all.at[s, c], dst_ref=w_all.at[s, c],
                send_sem=w_send.at[s, c, way], recv_sem=w_recv.at[s, c],
                device_id={"fsdp": target(way)}, device_id_type=MESH,
            )
        return make

    def own(make, act):
        s = me
        pl.when(z > 0)(lambda: act(make(s, LEFT)))
        pl.when(z < line - 1)(lambda: act(make(s, RIGHT)))
        act(make(s, PARTNER))

    def forward(make, k, act, wait):
        @pl.when(z >= k)
        def _():
            s = me - 2 * k
            if wait:
                make(s, PARTNER).wait_recv()
            pl.when(z < line - 1)(lambda: act(make(s, RIGHT)))
            act(make(s, PARTNER))

        @pl.when(z + k < line)
        def _():
            s = me + 2 * k
            if wait:
                make(s, PARTNER).wait_recv()
            pl.when(z > 0)(lambda: act(make(s, LEFT)))
            act(make(s, PARTNER))

    def start(copy):
        copy.start()

    def wait_send(copy):
        copy.wait_send()

    def piece(s, h):
        return pl.ds(pl.multiple_of(s * width + h * span, span), span)

    def a_copy(k, h):
        d = lax.rem(me + k, n)
        return pltpu.make_async_remote_copy(
            src_ref=acts_hbm.at[:, piece(d, h)], dst_ref=acts_t.at[h, me],
            send_sem=a_send.at[k, h], recv_sem=a_recv.at[me, h],
            device_id={"fsdp": d}, device_id_type=MESH,
        )

    def a_arrived(s, h):
        return pltpu.make_async_remote_copy(
            src_ref=acts_hbm.at[:, piece(s, h)], dst_ref=acts_t.at[h, s],
            send_sem=a_send.at[0, h], recv_sem=a_recv.at[s, h],
            device_id={"fsdp": lax.rem(me + 1, n)}, device_id_type=MESH,
        )

    load_og.wait()
    own(og_copy, start)

    for c in range(chunks):
        load_w(c).wait()
        own(w_copy(c), start)

    def send_acts(first, last):
        for h in range(first, last):
            @pl.loop(1, n)
            def _(k):
                a_copy(k, h).start()

    def ag_store(s):
        return pltpu.make_async_copy(ag.at[s], ag_hbm.at[:, cols(s)], ag_sem.at[s])

    def use_weight(s):
        for c in range(chunks):
            part = slice(c * rows, (c + 1) * rows)
            vals[...] += jnp.dot(acts[s, :, part], w_all[s, c], preferred_element_type=F32)
            ag[s, :, part] = lax.dot_general(
                og_all[me], w_all[s, c], (((1,), (1,)), ((), ())), preferred_element_type=F32
            ).astype(BF16)
        ag_store(s).start()

    def use_acts(a, s, h):
        wgrad[h] += lax.dot_general(
            a, og_all[s], (((0,), (0,)), ((), ())), preferred_element_type=F32
        )

    vals[...] = jnp.zeros_like(vals)
    wgrad[...] = jnp.zeros_like(wgrad)

    @pl.loop(0, n)
    def _(s):
        load_acts(s).wait()

    use_weight(me)
    for h in range(parts):
        use_acts(acts[me, :, h * span:(h + 1) * span], me, h)

    def gather(k):
        forward(og_copy, k, start, True)
        for c in range(chunks):
            forward(w_copy(c), k, start, True)

    def use_line(k):
        @pl.loop(0, 2)
        def _(j):
            zz = z + (1 - 2 * j) * k

            @pl.when((zz >= 0) & (zz < line))
            def _():
                use_weight(zz * 2 + y)

    def use_partner(k):
        @pl.loop(0, 2)
        def _(j):
            zz = z + (1 - 2 * j) * k

            @pl.when((zz >= 0) & (zz < line) & ((k > 0) | (j == 0)))
            def _():
                s = zz * 2 + 1 - y
                for c in range(chunks):
                    w_copy(c)(s, PARTNER).wait_recv()
                use_weight(s)

    gather(1)
    send_acts(0, (parts + 1) // 2)

    @pl.loop(2, line)
    def _(k):
        gather(k)
        pl.when(k == 2)(lambda: send_acts((parts + 1) // 2, parts))

    @pl.loop(0, line)
    def _(zz):
        og_copy(zz * 2 + 1 - y, PARTNER).wait_recv()

    def r_copy(k, h):
        d = lax.rem(rep + k, groups)
        return pltpu.make_async_remote_copy(
            src_ref=inner.at[h, d], dst_ref=rep_in.at[h, rep],
            send_sem=r_send.at[k, h], recv_sem=r_recv.at[rep, h],
            device_id={"rep": d}, device_id_type=MESH,
        )

    def r_arrived(k, h):
        d = lax.rem(rep + k, groups)
        return pltpu.make_async_remote_copy(
            src_ref=inner.at[h, d], dst_ref=rep_in.at[h, d],
            send_sem=r_send.at[k, h], recv_sem=r_recv.at[d, h],
            device_id={"rep": d}, device_id_type=MESH,
        )

    def o_copy(k, h):
        d = lax.rem(rep + k, groups)
        return pltpu.make_async_remote_copy(
            src_ref=outer_in.at[h, rep], dst_ref=outer_in.at[h, rep],
            send_sem=o_send.at[k, h], recv_sem=o_recv.at[rep, h],
            device_id={"rep": d}, device_id_type=MESH,
        )

    def o_arrived(k, h):
        d = lax.rem(rep + k, groups)
        return pltpu.make_async_remote_copy(
            src_ref=outer_in.at[h, d], dst_ref=outer_in.at[h, d],
            send_sem=o_send.at[k, h], recv_sem=o_recv.at[d, h],
            device_id={"rep": d}, device_id_type=MESH,
        )

    def inner_step(h):
        @pl.loop(1, n)
        def _(k):
            s = lax.rem(me + n - k, n)
            a_arrived(s, h).wait_recv()
            use_acts(acts_t[h, s], s, h)

        for j in range(groups):
            part = slice(j * block, (j + 1) * block)
            inner[h, j] = w_own[h, :, part].astype(F32) - rate * wgrad[h, :, part]
        for k in range(1, groups):
            r_copy(k, h).start()
        rep_in[h, rep] = inner[h, rep]

    def outer_step(h):
        across = slice(h * span, (h + 1) * span)
        for k in range(1, groups):
            r_arrived(k, h).wait_recv()
        total = rep_in[h, 0]
        for j in range(1, groups):
            total = total + rep_in[h, j]
        pseudo_grad = anchor[across] - total / groups
        mom_next = momentum_coef * mom[across] + pseudo_grad
        outer_in[h, rep] = (
            anchor[across] - outer_rate * (pseudo_grad + momentum_coef * mom_next)
        ).astype(BF16)
        for k in range(1, groups):
            o_copy(k, h).start()
        synced = jnp.full(mom_next.shape, plan[rep], jnp.int32) > 0
        new_mom_out[across] = jnp.where(synced, mom_next, mom[across])

    def last_step(h):
        across = slice(h * span, (h + 1) * span)
        for k in range(1, groups):
            o_arrived(k, h).wait_recv()
        for j in range(groups):
            synced = jnp.full(inner.shape[2:], plan[j], jnp.int32) > 0
            new_w_out[across, j * block:(j + 1) * block] = jnp.where(
                synced, outer_in[h, j].astype(F32), inner[h, j]
            ).astype(BF16)

    load_anchor.wait()
    load_mom.wait()
    for c in range(parts):
        load_own(c).wait()
    inner_step(0)
    for h in range(1, parts):
        inner_step(h)
        outer_step(h - 1)
    use_partner(0)

    @pl.loop(1, line - 1)
    def _(k):
        use_line(k)
        use_partner(k)

    use_line(line - 1)
    outer_step(parts - 1)
    for h in range(parts - 1):
        last_step(h)
    use_partner(line - 1)
    values_out[...] = vals[...].astype(BF16)
    last_step(parts - 1)

    own(og_copy, wait_send)
    for c in range(chunks):
        own(w_copy(c), wait_send)

    @pl.loop(1, line)
    def _(k):
        forward(og_copy, k, wait_send, False)
        for c in range(chunks):
            forward(w_copy(c), k, wait_send, False)

    @pl.loop(1, n)
    def _(k):
        for h in range(parts):
            a_copy(k, h).wait_send()

    for k in range(1, groups):
        for h in range(parts):
            r_copy(k, h).wait_send()
            o_copy(k, h).wait_send()

    @pl.loop(0, n)
    def _(s):
        ag_store(s).wait()


def local(n, groups, acts, out_grad, weights, anchor, momentum, plan):
    tokens, depth = acts.shape[1:]
    rows, kvw = weights.shape[1:]
    block = anchor.shape[1]
    rate = 1.0 / math.sqrt(tokens * n * depth)
    parts = max(1, min(8, rows // 128))
    chunks = max(1, min(4, rows // 256))
    span = rows // parts
    any_spec = pl.BlockSpec(memory_space=pl.ANY)
    vmem = pl.BlockSpec(memory_space=pltpu.VMEM)
    dma = pltpu.SemaphoreType.DMA
    values, act_grad, new_w, new_mom = pl.pallas_call(
        functools.partial(kernel, n, groups, chunks, rate),
        out_shape=(
            jax.ShapeDtypeStruct((tokens, kvw), BF16),
            jax.ShapeDtypeStruct((tokens, depth), BF16),
            jax.ShapeDtypeStruct((rows, kvw), BF16),
            jax.ShapeDtypeStruct((rows, block), F32),
        ),
        in_specs=[pl.BlockSpec(memory_space=pltpu.SMEM)] + [any_spec] * 5,
        out_specs=(vmem, any_spec, vmem, vmem),
        scratch_shapes=[
            pltpu.VMEM((n, tokens, rows), BF16),
            pltpu.VMEM((parts, n, tokens, span), BF16),
            pltpu.VMEM((n, tokens, kvw), BF16),
            pltpu.VMEM((n, chunks, rows // chunks, kvw), BF16),
            pltpu.VMEM((parts, span, kvw), BF16),
            pltpu.VMEM((n, tokens, rows), BF16),
            pltpu.VMEM((tokens, kvw), F32),
            pltpu.VMEM((parts, span, kvw), F32),
            pltpu.VMEM((parts, groups, span, block), F32),
            pltpu.VMEM((parts, groups, span, block), F32),
            pltpu.VMEM((parts, groups, span, block), BF16),
            pltpu.VMEM((rows, block), F32),
            pltpu.VMEM((rows, block), F32),
            dma((n,)), dma((1,)), dma((chunks,)), dma((2 + parts,)), dma((n,)),
            dma((n, 3)), dma((n,)), dma((n, chunks, 3)), dma((n, chunks)),
            dma((n, parts)), dma((n, parts)),
            dma((groups, parts)), dma((groups, parts)), dma((groups, parts)), dma((groups, parts)),
        ],
        compiler_params=pltpu.CompilerParams(
            collective_id=0, has_side_effects=True, vmem_limit_bytes=56 * 2**20
        ),
        cost_estimate=pl.CostEstimate(
            flops=6 * tokens * depth * kvw, bytes_accessed=24 * 2**20, transcendentals=0
        ),
    )(plan, acts[0], out_grad[0], weights[0], anchor, momentum)
    return values[None], act_grad[None], new_w[None], new_mom


def solution(mesh):
    placed = (
        P("rep", "fsdp", None),
        P("rep", "fsdp", None),
        P("rep", "fsdp", None),
        P("fsdp", "rep"),
        P("fsdp", "rep"),
        P(),
    )
    return jax.shard_map(
        functools.partial(local, mesh.shape["fsdp"], mesh.shape["rep"]),
        mesh=mesh,
        in_specs=placed,
        out_specs=(
            P("rep", "fsdp", None),
            P("rep", "fsdp", None),
            P("rep", "fsdp", None),
            P("fsdp", "rep"),
        ),
        check_vma=False,
    )
```
